32 devices in a mesh: dp: 8 (over y, x, core), section: 4 (over z).
Axes of the slice: x: 2, y: 2, z: 4, core: 2. Of those that a mesh axis runs over, the one named last changes fastest.
Arguments:
- saved_inputs: bfloat16 [4, 2, 48, 6144], P('section', None, 'dp'), may hold values from -6 to 6
- carried: bfloat16 [4, 48, 6144], P('section', 'dp'), may hold values from -6 to 6
- head_grad: bfloat16 [48, 6144], P('dp'), may hold values from -6 to 6
- routing: int32 [4, 2, 48, 2], P('section', None, 'dp'), may hold values from 0 to 7, as said below
- replica_counts: int32 [8], replicated, may hold values from 2 to 5
- router: float32 [4, 6144, 8], P('section'), may hold values from -0.21875 to 0.21875
- w_in: bfloat16 [4, 8, 1536, 4096], P('section', 'dp'), may hold values from -0.078125 to 0.078125
- w_out: bfloat16 [4, 8, 4096, 1536], P('section', 'dp'), may hold values from -0.0625 to 0.0625
Outputs:
- input_grad: bfloat16 [2, 4, 48, 6144], P(None, 'section', 'dp')
- grad_in: bfloat16 [4, 8, 1536, 4096], P('section', 'dp')
- grad_out: bfloat16 [4, 8, 4096, 1536], P('section', 'dp')
- grad_router: float32 [4, 6144, 8], P('section')
The draws below stay inside these ranges and needn't reach their ends.
Inputs may be any that keep to these rules, and one draw needn't show every extreme that they name: `routing`: each row names 2 different experts; in every section and step at most 2 of one device's 6 tokens name expert 0, and exactly 2 on some device.
All inputs are finite; a program needn't handle non-finite values.
Results may differ from the reference program's by a relative error of at most 0.0057.
Values may be sent and summed in bfloat16 or wider, within the bound.
No kernel may reach another device: no remote copies, remote signals or barrier semaphores. Data moves between devices by JAX's collectives and lax.ppermute only.
A program may use at most 128 MiB of HBM per device.

```python
import jax
import jax.numpy as jnp
from jax import lax

D = 6144
FF = 8192
EXPERTS = 8
TOP = 2
STEPS = 2
CAP = 2
TOK_DEV = 6
SECTIONS = 4
TOKENS = 48
GROUPS = 2
D_PART = 1536
HID_DEV = 4096
ROWS = 16
N_DP = 8


def draw_routing(key, part):
    keys = jax.random.split(key, 5)
    shape = (SECTIONS, STEPS, N_DP, TOK_DEV)
    base = jax.random.randint(keys[0], shape, 1, EXPERTS, dtype=jnp.int32)
    offset = jax.random.randint(keys[1], shape, 1, EXPERTS - 1, dtype=jnp.int32)
    second = 1 + (base - 1 + offset) % (EXPERTS - 1)
    count = jax.random.randint(keys[2], (SECTIONS, STEPS, N_DP), CAP // 2 + 1, CAP + 1, dtype=jnp.int32)
    fullest = jax.random.randint(keys[3], (SECTIONS, STEPS, 1), 0, N_DP, dtype=jnp.int32)
    count = jnp.where(jnp.arange(N_DP, dtype=jnp.int32)[None, None, :] == fullest, CAP, count)
    scores = jax.random.randint(keys[4], shape, 0, 1 << 20, dtype=jnp.int32) * TOK_DEV + jnp.arange(TOK_DEV, dtype=jnp.int32)
    order = jnp.argsort(scores, axis=3, stable=True)
    ranks = jnp.argsort(order, axis=3, stable=True).astype(jnp.int32)
    first = jnp.where(ranks < count[..., None], 0, base)
    return jnp.stack([first, second], axis=-1).reshape(SECTIONS, STEPS, TOKENS, TOP).astype(jnp.int32)


def touch_ends(result, key, low, largest):
    place = [jax.random.randint(jax.random.fold_in(key, axis), (), 0, length) for axis, length in enumerate(result.shape)]
    widest = result.shape.index(max(result.shape))
    beside = place[:widest] + [(place[widest] + 1) % result.shape[widest]] + place[widest + 1:]
    return result.at[tuple(place)].set(low).at[tuple(beside)].set(largest)


def block_levels(key, shape, cuts, low, largest):
    level, own = 1.0, jax.random.fold_in(key, 6)
    for axis_at, parts in cuts:
        heights = jnp.exp(jax.random.uniform(jax.random.fold_in(own, axis_at), (parts,), jnp.float32, low / len(cuts), largest / len(cuts)))
        level = level * jnp.repeat(heights, shape[axis_at] // parts).reshape([-1 if axis == axis_at else 1 for axis in range(len(shape))])
    return level


def noise(rng, shape, spread, most, shards=(), kind=jnp.bfloat16):
    values = jax.random.normal(rng, shape, jnp.float32) * spread
    if len(shards) > 0:
        values = block_levels(rng, shape, shards, -0.22, 0.18) * values
    return jnp.clip(values, min=-most, max=most).astype(kind)


def setup_inputs(seed: int = 0) -> dict:
    arg_keys = jax.random.split(jax.random.key(seed), 9)
    saved_inputs = noise(arg_keys[0], (SECTIONS, STEPS, TOKENS, D), 1.0, 6.0, ((0, 4), (2, 8)))
    carried = noise(arg_keys[1], (SECTIONS, TOKENS, D), 1.0, 6.0, ((0, 4), (1, 8)))
    head_grad = noise(arg_keys[2], (TOKENS, D), 1.0, 6.0, ((0, 8),))
    routing = draw_routing(jax.random.fold_in(arg_keys[8], 71), 0)
    replica_counts = touch_ends(jax.random.randint(arg_keys[4], (N_DP,), 2, SECTIONS + 2), jax.random.fold_in(arg_keys[4], 1), 2, (SECTIONS + 2) - 1).astype(jnp.int32)
    router = noise(arg_keys[5], (SECTIONS, D, EXPERTS), (D // 9) ** -0.5, 0.21875, ((0, 4),), jnp.float32)
    w_in = noise(arg_keys[6], (SECTIONS, N_DP, D_PART, HID_DEV), D ** -0.5, 0.078125, ((0, 4), (1, 8)))
    w_out = noise(arg_keys[7], (SECTIONS, N_DP, HID_DEV, D_PART), FF ** -0.5, 0.0625, ((0, 4), (1, 8)))
    return {"saved_inputs": saved_inputs, "carried": carried, "head_grad": head_grad, "routing": routing, "replica_counts": replica_counts, "router": router, "w_in": w_in, "w_out": w_out}


def silu_grad(value):
    sig = jax.nn.sigmoid(value)
    return sig * (1.0 + value * (1.0 - sig))

def full_in(block):
    return block.reshape(GROUPS, 4, D_PART, HID_DEV).transpose(1, 2, 0, 3).reshape(D, FF)

def block_in(full):
    return full.reshape(4, D_PART, GROUPS, HID_DEV).transpose(2, 0, 1, 3).reshape(N_DP, D_PART, HID_DEV)

def full_out(block):
    return block.reshape(GROUPS, 4, HID_DEV, D_PART).transpose(0, 2, 1, 3).reshape(FF, D)

def block_out(full):
    return full.reshape(GROUPS, HID_DEV, 4, D_PART).transpose(0, 2, 1, 3).reshape(N_DP, HID_DEV, D_PART)

def slot_table(ids, live_tok):
    routed = ((ids[:, 0] == 0) | (ids[:, 1] == 0)) & live_tok
    flags = routed.reshape(N_DP, TOK_DEV).astype(jnp.int32)
    slot = jnp.cumsum(flags, axis=1, dtype=jnp.int32) - 1
    slots = jnp.arange(CAP, dtype=jnp.int32)
    table = (slot[:, None, :] == slots[None, :, None]) & (flags[:, None, :] == 1)
    return table.astype(jnp.float32)

def section_back(xin, incoming, ids, live_rep, router_w, weight_in, weight_out):
    hi = lax.Precision.HIGHEST
    live_tok = jnp.repeat(live_rep, TOK_DEV)
    dy = jnp.where(live_tok[:, None], incoming, jnp.zeros_like(incoming))
    xf = xin.astype(jnp.float32)
    logits = jnp.dot(xf, router_w, precision=hi)
    expo = jnp.exp(logits)
    prob = expo / lax.optimization_barrier(jnp.sum(expo, axis=1, keepdims=True))
    table = slot_table(ids, live_tok)
    xs = jnp.einsum('jct,jtd->jcd', table, xf.reshape(N_DP, TOK_DEV, D), precision=hi).reshape(ROWS, D).astype(jnp.bfloat16)
    ys = jnp.einsum('jct,jtd->jcd', table, dy.astype(jnp.float32).reshape(N_DP, TOK_DEV, D), precision=hi).reshape(ROWS, D).astype(jnp.bfloat16)
    gate = jnp.einsum('jct,jt->jc', table, prob[:, 0].reshape(N_DP, TOK_DEV), precision=hi).reshape(ROWS).astype(jnp.bfloat16)
    pre = jnp.dot(xs, weight_in, preferred_element_type=jnp.float32)
    upper = lax.dot_general(ys, weight_out, (((1,), (1,)), ((), ())), preferred_element_type=jnp.float32)
    act = jax.nn.silu(pre)
    gate_f = gate.astype(jnp.float32)[:, None]
    dpre = (gate_f * upper * silu_grad(pre)).astype(jnp.bfloat16)
    scaled = (gate_f * act).astype(jnp.bfloat16)
    block_sums = lax.optimization_barrier(jnp.sum((act * upper).reshape(ROWS, GROUPS, HID_DEV), axis=2))
    block_sums = lax.optimization_barrier(block_sums.astype(jnp.bfloat16)).astype(jnp.float32)
    dgate = lax.optimization_barrier(jnp.sum(block_sums, axis=1))

    def group_term(total, group):
        piece = lax.dynamic_slice_in_dim(dpre, group * HID_DEV, HID_DEV, 1)
        wpiece = lax.dynamic_slice_in_dim(weight_in, group * HID_DEV, HID_DEV, 1)
        term = lax.dot_general(piece, wpiece, (((1,), (1,)), ((), ())), preferred_element_type=jnp.float32)
        term = lax.optimization_barrier(term.astype(jnp.bfloat16)).astype(jnp.float32)
        return (total + term, None)
    dxs, _ = lax.scan(group_term, jnp.zeros((ROWS, D), jnp.float32), jnp.arange(GROUPS, dtype=jnp.int32))
    grad_one = lax.dot_general(xs, dpre, (((0,), (0,)), ((), ())), preferred_element_type=jnp.float32)
    grad_two = lax.dot_general(scaled, ys, (((0,), (0,)), ((), ())), preferred_element_type=jnp.float32)
    dxe = jnp.einsum('jct,jcd->jtd', table, dxs.reshape(N_DP, CAP, D), precision=hi).reshape(TOKENS, D)
    dg_tok = jnp.einsum('jct,jc->jt', table, dgate.reshape(N_DP, CAP), precision=hi).reshape(TOKENS)
    first = (jnp.arange(EXPERTS, dtype=jnp.int32) == 0).astype(jnp.float32)
    dlog = (dg_tok * prob[:, 0])[:, None] * (first[None, :] - prob)
    dx = dy.astype(jnp.float32) + dxe + jnp.dot(dlog, router_w.T, precision=hi)
    grad_r = jnp.dot(xf.T, dlog, precision=hi)
    return (dx.astype(jnp.bfloat16), grad_one, grad_two, grad_r)

def reference(saved_inputs, carried, head_grad, routing, replica_counts, router, w_in, w_out):
    first_dx = []
    totals = []
    for section in range(SECTIONS):
        weight_in = full_in(w_in[section])
        weight_out = full_out(w_out[section])
        live_rep = section < replica_counts
        out = section_back(saved_inputs[section, 0], carried[section], routing[section, 0], live_rep, router[section], weight_in, weight_out)
        first_dx.append(out[0])
        totals.append(out[1:])
    second_dx = [None] * SECTIONS
    grads_in = [None] * SECTIONS
    grads_out = [None] * SECTIONS
    grads_r = [None] * SECTIONS
    for section in range(SECTIONS - 1, -1, -1):
        weight_in = full_in(w_in[section])
        weight_out = full_out(w_out[section])
        incoming = head_grad if section == SECTIONS - 1 else first_dx[section + 1]
        live_rep = section + 1 < replica_counts
        out = section_back(saved_inputs[section, 1], incoming, routing[section, 1], live_rep, router[section], weight_in, weight_out)
        second_dx[section] = out[0]
        grads_in[section] = block_in((totals[section][0] + out[1]).astype(jnp.bfloat16))
        grads_out[section] = block_out((totals[section][1] + out[2]).astype(jnp.bfloat16))
        grads_r[section] = totals[section][2] + out[3]
    input_grad = jnp.stack([jnp.stack(first_dx), jnp.stack(second_dx)])
    return (input_grad, jnp.stack(grads_in), jnp.stack(grads_out), jnp.stack(grads_r))
```

```python
import functools

import jax
import jax.numpy as jnp
from jax import lax
from jax.experimental import pallas as pl
from jax.experimental.pallas import tpu as pltpu
from jax.sharding import PartitionSpec as P

STEPS = 2
CAP = 2
QUARTERS = 4
LANES = 128
SLAB = 8
BF = jnp.bfloat16
F32 = jnp.float32
MIB = 1 << 20

NN = (((1,), (0,)), ((), ()))
NT = (((1,), (1,)), ((), ()))
TN = (((0,), (0,)), ((), ()))

VMEM = pl.BlockSpec(memory_space=pltpu.VMEM)
SMEM = pl.BlockSpec(memory_space=pltpu.SMEM)
ANY = pl.BlockSpec(memory_space=pl.ANY)


def dot(a, b, dims=NN):
    return lax.dot_general(a, b, dims, preferred_element_type=F32)


def dot_hi(a, b, dims=NN):
    return lax.dot_general(
        a, b, dims, preferred_element_type=F32, precision=lax.Precision.HIGHEST
    )


def iota(shape, dim):
    return lax.broadcasted_iota(jnp.int32, shape, dim)


def one_hot(cond):
    return jnp.where(cond, 1.0, 0.0).astype(BF)


def sds(shape, dtype):
    return jax.ShapeDtypeStruct(shape, dtype)


def call(body, args, specs, outs, flops=0, data=0, limit=12, scratch=(), out_specs=None):
    many = isinstance(outs, tuple)
    if out_specs is None:
        out_specs = tuple(VMEM for _ in outs) if many else VMEM
    return pl.pallas_call(
        body,
        in_specs=specs,
        out_specs=out_specs,
        out_shape=outs,
        scratch_shapes=scratch,
        cost_estimate=pl.CostEstimate(flops=flops, bytes_accessed=data, transcendentals=0),
        compiler_params=pltpu.CompilerParams(vmem_limit_bytes=limit * MIB),
    )(*args)


def in_vmem(weight):
    return pltpu.with_memory_space_constraint(weight, pltpu.VMEM)


def chunk_of(size, most):
    while size % most:
        most //= 2
    return most


def permuted(array, bit):
    count = lax.axis_size("dp")
    return lax.ppermute(array, "dp", [(i, i ^ (1 << bit)) for i in range(count)])


def from_next_section(array):
    count = lax.axis_size("section")
    return lax.ppermute(array, "section", [(i + 1, i) for i in range(count - 1)])


def slot_tokens(ids, step, live):
    tokens = ids.shape[2]
    count = jnp.int32(0)
    held = [jnp.int32(-1)] * CAP
    for t in range(tokens):
        routed = ((ids[step, 0, t] == 0) | (ids[step, 1, t] == 0)) & live
        for c in range(CAP):
            held[c] = jnp.where(routed & (count == c), jnp.int32(t), held[c])
        count = count + routed.astype(jnp.int32)
    return held


def silu_parts(pre):
    sig = jax.nn.sigmoid(pre)
    return pre * sig, sig * (1.0 + pre * (1.0 - sig))


def softmax_rows(logits, experts):
    lane = iota(logits.shape, 1)
    expo = jnp.where(lane < experts, jnp.exp(logits), 0.0)
    return expo / jnp.sum(expo, axis=1, keepdims=True)


def first_minus(prob):
    lane = iota(prob.shape, 1)
    return jnp.where(lane == 0, 1.0, 0.0) - prob


def local(saved_inputs, carried, head_grad, routing, replica_counts, router, w_in, w_out):
    sections = lax.axis_size("section")
    n = lax.axis_size("dp")
    groups = n // QUARTERS
    width = head_grad.shape[1]
    tokens = head_grad.shape[0]
    part = w_in.shape[2]
    hidden = w_in.shape[3]
    half = hidden // 2
    experts = router.shape[2]
    rows = n * CAP
    w1 = in_vmem(w_in[0, 0])
    w2 = in_vmem(w_out[0, 0])
    router_t = router[0].T
    x_tok = saved_inputs[0].transpose(1, 0, 2)
    carried_tok = carried[0]
    ids = routing[0].transpose(0, 2, 1)
    last_section = sections - 1

    def where_am_i():
        return lax.axis_index("section"), lax.axis_index("dp")

    def quarter_lanes():
        return pl.ds(pl.multiple_of(lax.rem(lax.axis_index("dp"), QUARTERS) * part, LANES), part)

    def half_lanes(core):
        return pl.ds(pl.multiple_of(core * half, LANES), half)

    def pick(held, value):
        row = iota((SLAB, value.shape[0]), 0)
        col = iota((SLAB, value.shape[0]), 1)
        chosen = jnp.zeros((SLAB, value.shape[0]), F32)
        for c in range(len(held)):
            chosen = chosen + jnp.where((row == c) & (col == held[c]), 1.0, 0.0)
        return dot(chosen.astype(BF), value)

    def send_quarters(slab, out_ref):
        for q in range(QUARTERS):
            piece = slab[:, q * part:(q + 1) * part]
            for g in range(groups):
                out_ref[g * QUARTERS + q] = piece

    def dispatch_body(ids_ref, counts_ref, x_ref, dy_ref, out_ref):
        section, dev = where_am_i()
        count = counts_ref[dev]
        held = [slot_tokens(ids_ref, step, step + section < count) for step in range(STEPS)]
        slab = pick([-1] * (STEPS * CAP) + held[0], dy_ref[...])
        row = iota((SLAB, width), 0)
        for step in range(STEPS):
            for c in range(CAP):
                value = x_ref[jnp.maximum(held[step][c], 0), step:step + 1, :].astype(F32)
                wanted = (row == step * CAP + c) & (held[step][c] >= 0)
                slab = jnp.where(wanted, jnp.broadcast_to(value, (SLAB, width)), slab)
        send_quarters(slab.astype(BF), out_ref)

    sent = call(
        dispatch_body,
        (ids, replica_counts, x_tok, carried_tok),
        [SMEM, SMEM, VMEM, VMEM],
        sds((n, SLAB, part), BF),
        data=4 * MIB,
    )
    carried_next = from_next_section(carried_tok)
    ids_next = from_next_section(ids)
    came = lax.all_to_all(sent, "dp", split_axis=0, concat_axis=0, tiled=True)

    wide = half + LANES

    def first_body(came_ref, w1_ref, w2_ref, router_ref, xs_ref, ys_ref, keep_ref, send_ref):
        core = lax.rem(lax.axis_index("dp"), 2)
        flat = came_ref[...].reshape(n * SLAB, part)
        row = iota((STEPS * rows, n * SLAB), 0)
        col = iota((STEPS * rows, n * SLAB), 1)
        slot = row % rows
        want = (slot // CAP) * SLAB + (row // rows) * CAP + slot % CAP
        xs = dot(one_hot(col == want), flat).astype(BF)
        row = iota((rows, n * SLAB), 0)
        col = iota((rows, n * SLAB), 1)
        ys = dot(one_hot(col == (row // CAP) * SLAB + 2 * CAP + row % CAP), flat).astype(BF)
        xs_ref[...] = xs
        ys_ref[...] = ys
        logits = dot_hi(xs.astype(F32), router_ref[:, quarter_lanes()], NT)
        logits = jnp.concatenate(
            [logits, jnp.zeros((STEPS * rows, LANES - experts), F32)], axis=1
        )
        zero = jnp.zeros((rows, LANES), F32)
        both = STEPS * rows
        step = chunk_of(half, 512)
        for ref, which in ((send_ref, 1 - core), (keep_ref, core)):
            for at in range(0, half, step):
                lanes = pl.ds(pl.multiple_of(which * half + at, LANES), step)
                ref[0:both, at:at + step] = dot(xs, w1_ref[:, lanes])
            for at in range(0, half, step):
                lanes = pl.ds(pl.multiple_of(which * half + at, LANES), step)
                ref[both:both + rows, at:at + step] = dot(ys, w2_ref[lanes, :], NT)
            ref[0:both, half:wide] = logits
            ref[both:both + rows, half:wide] = zero

    xs, ys0, keep, send = call(
        first_body,
        (came, w1, w2, router_t),
        [VMEM] * 4,
        (
            sds((STEPS * rows, part), BF),
            sds((rows, part), BF),
            sds((3 * rows, wide), F32),
            sds((3 * rows, wide), F32),
        ),
        flops=2 * 3 * rows * part * hidden,
        data=2 * part * hidden * 2,
    )
    pair = keep + permuted(send, 0)
    mine0 = jnp.concatenate([pair[0:rows], pair[2 * rows:3 * rows]], axis=0)
    mine1 = pair[rows:2 * rows]
    other0 = permuted(mine0, 1)

    def gated(pre, upper, gate):
        act, slope = silu_parts(pre)
        dpre = (gate * upper * slope).astype(BF)
        block = jnp.sum(act * upper, axis=1, keepdims=True)
        return act, dpre, block

    def split_sum(block):
        high = block.astype(BF)
        low = (block - high.astype(F32)).astype(BF)
        lane = iota((rows, LANES), 1)
        zero = jnp.zeros((rows, LANES), BF)
        return jnp.where(lane == 0, high, jnp.where(lane == 1, low, zero))

    def gate_of(prob):
        return prob[:, 0:1].astype(BF).astype(F32)

    def act0_body(a_ref, b_ref, out_ref, prob_ref, block_ref):
        prob = softmax_rows(a_ref[0:rows, half:wide] + b_ref[0:rows, half:wide], experts)
        gate = gate_of(prob)
        pre = a_ref[0:rows, 0:half] + b_ref[0:rows, 0:half]
        upper = a_ref[rows:2 * rows, 0:half] + b_ref[rows:2 * rows, 0:half]
        act, dpre, block = gated(pre, upper, gate)
        out_ref[:, 0:half] = dpre
        out_ref[:, half:wide] = split_sum(block)
        out_ref[:, wide:wide + half] = (gate * act).astype(BF)
        prob_ref[...] = prob
        block_ref[...] = jnp.broadcast_to(block, (rows, LANES))

    hid0, prob0, block0 = call(
        act0_body,
        (mine0, other0),
        [VMEM] * 2,
        (sds((rows, wide + half), BF), sds((rows, LANES), F32), sds((rows, LANES), F32)),
    )
    hid0_pair = permuted(hid0, 0)

    def block_sum(block, pair_ref):
        extra = pair_ref[:, half:half + 1].astype(F32) + pair_ref[:, half + 1:half + 2].astype(F32)
        return (block[:, 0:1] + extra).astype(BF)

    def in_order(own, pair, core):
        return (
            jnp.where(core == 0, own, pair),
            jnp.where(core == 0, pair, own),
        )

    def dx_of(own_ref, pair_ref, w1_ref, core):
        low, high = in_order(own_ref[:, 0:half], pair_ref[:, 0:half], core)
        step = chunk_of(part, 256)
        pieces = []
        for at in range(0, part, step):
            pieces.append(
                dot(low, w1_ref[at:at + step, 0:half], NT)
                + dot(high, w1_ref[at:at + step, half:hidden], NT)
            )
        return jnp.concatenate(pieces, axis=1)

    def dx0_body(own_ref, pair_ref, block_ref, w1_ref, out_ref):
        core = lax.rem(lax.axis_index("dp"), 2)
        out_ref[:, 0:part] = dx_of(own_ref, pair_ref, w1_ref, core).astype(BF)
        dgate = block_sum(block_ref[...], pair_ref)
        lane = iota((rows, LANES), 1)
        out_ref[:, part:part + LANES] = jnp.where(
            lane == 0, jnp.broadcast_to(dgate, (rows, LANES)), jnp.zeros((rows, LANES), BF)
        )

    dx0 = call(
        dx0_body,
        (hid0, hid0_pair, block0, w1),
        [VMEM] * 4,
        sds((rows, part + LANES), BF),
        flops=2 * rows * part * hidden,
        data=2 * part * hidden,
    )
    total0, bit = dx0, 2
    while (1 << (bit + 1)) < n:
        total0 = total0.astype(F32) + permuted(total0, bit).astype(F32)
        bit += 1
    other_total0 = permuted(total0, bit) if groups > 1 else jnp.zeros_like(total0)

    def sum0_body(a_ref, b_ref, prob_ref, router_ref, out_ref, dlog_ref):
        total = a_ref[...].astype(F32) + b_ref[...].astype(F32)
        prob = prob_ref[...]
        dlog = total[:, part:part + 1] * prob[:, 0:1] * first_minus(prob)
        dlog_ref[...] = dlog
        back = dot_hi(dlog[:, 0:experts], router_ref[:, quarter_lanes()])
        out_ref[...] = (total[:, 0:part] + back).astype(BF)

    dxs0, dlog0 = call(
        sum0_body,
        (total0, other_total0, prob0, router_t),
        [VMEM] * 4,
        (sds((rows, part), BF), sds((rows, LANES), F32)),
    )
    dxs_next = from_next_section(dxs0)

    def base_body(ids_ref, next_ref, counts_ref, dy_ref, head_ref, out_ref):
        section, dev = where_am_i()
        live = 1 + section < counts_ref[dev]
        last = section == last_section
        held = slot_tokens(ids_ref, 1, live)
        before = slot_tokens(next_ref, 0, live & jnp.logical_not(last))
        slab = pick(held, jnp.where(last, head_ref[...], dy_ref[...]))
        row = iota((SLAB, width), 0)
        lane = lax.rem(iota((SLAB, width), 1), part)
        for c in range(CAP):
            for b in range(CAP):
                same = (held[c] >= 0) & (held[c] == before[b])
                slab = jnp.where((row == CAP + c) & (lane == b) & same, 1.0, slab)
        send_quarters(slab.astype(BF), out_ref)

    base_sent = call(
        base_body,
        (ids, ids_next, replica_counts, carried_next, head_grad),
        [SMEM, SMEM, SMEM, VMEM, VMEM],
        sds((n, SLAB, part), BF),
        data=4 * MIB,
    )
    base = lax.all_to_all(base_sent, "dp", split_axis=0, concat_axis=0, tiled=True)
    other1 = permuted(mine1, 1)

    def up1_body(base_ref, dxs_ref, w2_ref, ys_ref, keep_ref, send_ref):
        core = lax.rem(lax.axis_index("dp"), 2)
        flat = base_ref[...].reshape(n * SLAB, part)
        row = iota((rows, n * SLAB), 0)
        col = iota((rows, n * SLAB), 1)
        want = (row // CAP) * SLAB + row % CAP
        value = dot(one_hot(col == want), flat)
        match = dot(one_hot(col == want + CAP), flat[:, 0:LANES])
        row = iota((rows, rows), 0)
        col = iota((rows, rows), 1)
        place = jnp.zeros((rows, rows), F32)
        for b in range(CAP):
            place = place + jnp.where(
                (row // CAP == col // CAP) & (col % CAP == b), match[:, b:b + 1], 0.0
            )
        ys = (value + dot(place.astype(BF), dxs_ref[...])).astype(BF)
        ys_ref[...] = ys
        step = chunk_of(half, 512)
        for ref, which in ((send_ref, 1 - core), (keep_ref, core)):
            for at in range(0, half, step):
                lanes = pl.ds(pl.multiple_of(which * half + at, LANES), step)
                ref[:, at:at + step] = dot(ys, w2_ref[lanes, :], NT)

    ys1, keep1, send1 = call(
        up1_body,
        (base, dxs_next, w2),
        [VMEM] * 3,
        (sds((rows, part), BF), sds((rows, half), F32), sds((rows, half), F32)),
        flops=2 * rows * part * hidden,
        data=2 * part * hidden,
    )
    up1 = keep1 + permuted(send1, 0)
    other_up1 = permuted(up1, 1)

    def act1_body(a_ref, b_ref, out_ref, prob_ref):
        prob = softmax_rows(a_ref[:, half:wide] + b_ref[:, half:wide], experts)
        act, _ = silu_parts(a_ref[:, 0:half] + b_ref[:, 0:half])
        out_ref[...] = (gate_of(prob) * act).astype(BF)
        prob_ref[...] = prob

    scaled1, prob1 = call(
        act1_body,
        (mine1, other1),
        [VMEM] * 2,
        (sds((rows, half), BF), sds((rows, LANES), F32)),
    )
    scaled1_pair = permuted(scaled1, 0)

    both = STEPS * rows

    def outer(body, args, height, across, flops):
        return call(
            body,
            args,
            [VMEM] * len(args),
            sds((height, across), BF),
            flops=flops,
            data=2 * height * across,
            limit=22,
            out_specs=ANY,
            scratch=[
                pltpu.VMEM((height, across), BF),
                pltpu.SemaphoreType.DMA((SLAB,)),
            ],
        )

    def write_out(a, b, out_ref, held_ref, sems):
        height = held_ref.shape[0]
        step = height // SLAB
        copies = []
        for i in range(SLAB):
            at = pl.ds(i * step, step)
            held_ref[i * step:(i + 1) * step, :] = dot(
                a[:, i * step:(i + 1) * step], b, TN
            ).astype(BF)
            copy = pltpu.make_async_copy(held_ref.at[at], out_ref.at[at], sems.at[i])
            copy.start()
            copies.append(copy)
        for copy in copies:
            copy.wait()

    def grad_out_body(own0, pair0, own1, pair1, ys0_ref, ys1_ref, out_ref, held_ref, sems):
        core = lax.rem(lax.axis_index("dp"), 2)
        a0, b0 = in_order(own0[:, wide:wide + half], pair0[:, wide:wide + half], core)
        a1, b1 = in_order(own1[...], pair1[...], core)
        scaled = jnp.concatenate(
            [jnp.concatenate([a0, b0], axis=1), jnp.concatenate([a1, b1], axis=1)], axis=0
        )
        ys = jnp.concatenate([ys0_ref[...], ys1_ref[...]], axis=0)
        write_out(scaled, ys, out_ref, held_ref, sems)

    grad_out = outer(
        grad_out_body,
        (hid0, hid0_pair, scaled1, scaled1_pair, ys0, ys1),
        hidden,
        part,
        2 * both * part * hidden,
    )

    def act2_body(a_ref, b_ref, up_ref, other_ref, prob_ref, out_ref, block_ref):
        pre = a_ref[:, 0:half] + b_ref[:, 0:half]
        upper = up_ref[...] + other_ref[...]
        _, dpre, block = gated(pre, upper, gate_of(prob_ref[...]))
        out_ref[:, 0:half] = dpre
        out_ref[:, half:wide] = split_sum(block)
        block_ref[...] = jnp.broadcast_to(block, (rows, LANES))

    hid1, block1 = call(
        act2_body,
        (mine1, other1, up1, other_up1, prob1),
        [VMEM] * 5,
        (sds((rows, wide), BF), sds((rows, LANES), F32)),
    )
    hid1_pair = permuted(hid1, 0)

    back_rows = 2 * SLAB

    def dx1_body(
        own_ref, pair_ref, block_ref, prob_ref, dlog0_ref, xs_ref, dxs0_ref, next_ref, router_ref, w1_ref, out_ref
    ):
        dev = lax.axis_index("dp")
        core = lax.rem(dev, 2)
        group = dev // QUARTERS
        dx = dx_of(own_ref, pair_ref, w1_ref, core)
        prob = prob_ref[...]
        dgate = block_sum(block_ref[...], pair_ref).astype(F32)
        dlog = dgate * prob[:, 0:1] * first_minus(prob)
        dx = (dx + dot_hi(dlog[:, 0:experts], router_ref[:, quarter_lanes()])).astype(BF)
        aux = jnp.where(group == 0, dxs0_ref[...], next_ref[...])
        dlogs = jnp.concatenate(
            [jnp.where(group == 0, dlog0_ref[...], 0.0), dlog], axis=0
        )
        grad = dot_hi(dlogs, xs_ref[...].astype(F32), TN)[0:experts, :].astype(BF)
        source = jnp.concatenate([dx, aux, grad], axis=0)
        count = 2 * rows + experts
        row = iota((n * back_rows, count), 0)
        col = iota((n * back_rows, count), 1)
        home = row // back_rows
        kind = row % back_rows
        want = jnp.where(
            kind < 2 * CAP,
            (kind // CAP) * rows + home * CAP + kind % CAP,
            jnp.where(kind >= SLAB, 2 * rows + kind - SLAB, -1),
        )
        out_ref[...] = dot(one_hot(col == want), source).astype(BF).reshape(n, back_rows, part)

    back_sent = call(
        dx1_body,
        (hid1, hid1_pair, block1, prob1, dlog0, xs, dxs0, dxs_next, router_t, w1),
        [VMEM] * 10,
        sds((n, back_rows, part), BF),
        flops=2 * rows * part * hidden,
        data=2 * part * hidden,
        limit=16,
    )
    back = lax.all_to_all(back_sent, "dp", split_axis=0, concat_axis=0, tiled=True)

    def grad_in_body(own0, pair0, own1, pair1, xs_ref, out_ref, held_ref, sems):
        core = lax.rem(lax.axis_index("dp"), 2)
        a0, b0 = in_order(own0[:, 0:half], pair0[:, 0:half], core)
        a1, b1 = in_order(own1[:, 0:half], pair1[:, 0:half], core)
        dpre = jnp.concatenate(
            [jnp.concatenate([a0, b0], axis=1), jnp.concatenate([a1, b1], axis=1)], axis=0
        )
        write_out(xs_ref[...], dpre, out_ref, held_ref, sems)

    grad_in = outer(
        grad_in_body,
        (hid0, hid0_pair, hid1, hid1_pair, xs),
        part,
        hidden,
        2 * both * part * hidden,
    )

    def final_body(
        ids_ref, next_ids_ref, counts_ref, back_ref, dy_ref, dy_next_ref, head_ref, out_ref, router_out_ref
    ):
        section, dev = where_am_i()
        count = counts_ref[dev]
        last = section == last_section
        live0 = section < count
        live1 = 1 + section < count
        held0 = slot_tokens(ids_ref, 0, live0)
        held1 = slot_tokens(ids_ref, 1, live1)
        before = slot_tokens(next_ids_ref, 0, live1 & jnp.logical_not(last))
        wide_dy = jnp.where(live0, dy_ref[...].astype(F32), 0.0)
        dy1 = jnp.where(last, head_ref[...].astype(F32), dy_next_ref[...].astype(F32))
        wide_dy1 = jnp.where(live1, dy1, 0.0)

        def put(held, at, value):
            row = iota((tokens, 2 * SLAB), 0)
            col = iota((tokens, 2 * SLAB), 1)
            place = jnp.zeros((tokens, 2 * SLAB), F32)
            for c in range(CAP):
                place = place + jnp.where((row == held[c]) & (col == at + c), 1.0, 0.0)
            return dot(place.astype(BF), value)

        for q in range(QUARTERS):
            lanes = slice(q * part, (q + 1) * part)
            blocks = [back_ref[g * QUARTERS + q] for g in range(groups)]
            grad = blocks[0][SLAB:SLAB + experts].astype(F32)
            for block in blocks[1:]:
                grad = grad + block[SLAB:SLAB + experts].astype(F32)
            router_out_ref[:, lanes] = grad
            out0 = wide_dy[:, lanes] + put(held0, CAP, blocks[0])
            out1 = wide_dy1[:, lanes]
            if groups > 1:
                out1 = out1 + put(before, CAP, blocks[1])
            out1 = out1.astype(BF).astype(F32)
            for block in blocks:
                out1 = out1 + put(held1, 0, block)
            out0 = out0.astype(BF)
            out1 = out1.astype(BF)
            for t in range(tokens):
                out_ref[t, 0:1, lanes] = out0[t:t + 1]
                out_ref[t, 1:2, lanes] = out1[t:t + 1]

    grads, router_grad = call(
        final_body,
        (ids, ids_next, replica_counts, back, carried_tok, carried_next, head_grad),
        [SMEM, SMEM, SMEM, VMEM, VMEM, VMEM, VMEM],
        (sds((tokens, STEPS, width), BF), sds((experts, width), F32)),
        limit=24,
    )
    input_grad = grads.transpose(1, 0, 2)[:, None]
    return (input_grad, grad_in[None, None], grad_out[None, None], router_grad.T[None])


def solution(mesh):
    in_specs = (
        P("section", None, "dp", None),
        P("section", "dp", None),
        P("dp", None),
        P("section", None, "dp", None),
        P(),
        P("section", None, None),
        P("section", "dp", None, None),
        P("section", "dp", None, None),
    )
    out_specs = (
        P(None, "section", "dp", None),
        P("section", "dp", None, None),
        P("section", "dp", None, None),
        P("section", None, None),
    )
    return jax.shard_map(local, mesh=mesh, in_specs=in_specs, out_specs=out_specs, check_vma=False)
```

```python
import functools

import jax
import jax.numpy as jnp
from jax import lax
from jax.experimental import pallas as pl
from jax.experimental.pallas import tpu as pltpu
from jax.sharding import PartitionSpec as P

STEPS = 2
CAP = 2
QUARTERS = 4
LANES = 128
SLAB = 8
BF = jnp.bfloat16
F32 = jnp.float32
MIB = 1 << 20

NN = (((1,), (0,)), ((), ()))
NT = (((1,), (1,)), ((), ()))
TN = (((0,), (0,)), ((), ()))

VMEM = pl.BlockSpec(memory_space=pltpu.VMEM)
SMEM = pl.BlockSpec(memory_space=pltpu.SMEM)
ANY = pl.BlockSpec(memory_space=pl.ANY)


def dot(a, b, dims=NN):
    return lax.dot_general(a, b, dims, preferred_element_type=F32)


def dot_hi(a, b, dims=NN):
    return lax.dot_general(
        a, b, dims, preferred_element_type=F32, precision=lax.Precision.HIGHEST
    )


def iota(shape, dim):
    return lax.broadcasted_iota(jnp.int32, shape, dim)


def one_hot(cond):
    return jnp.where(cond, 1.0, 0.0).astype(BF)


def sds(shape, dtype):
    return jax.ShapeDtypeStruct(shape, dtype)


def call(body, args, specs, outs, flops=0, data=0, limit=12, scratch=(), out_specs=None):
    many = isinstance(outs, tuple)
    if out_specs is None:
        out_specs = tuple(VMEM for _ in outs) if many else VMEM
    return pl.pallas_call(
        body,
        in_specs=specs,
        out_specs=out_specs,
        out_shape=outs,
        scratch_shapes=scratch,
        cost_estimate=pl.CostEstimate(flops=flops, bytes_accessed=data, transcendentals=0),
        compiler_params=pltpu.CompilerParams(vmem_limit_bytes=limit * MIB),
    )(*args)


def in_hbm(array):
    return pltpu.with_memory_space_constraint(array, pltpu.HBM)


def copy_all(pairs, sems):
    copies = [
        pltpu.make_async_copy(source, target, sems.at[i])
        for i, (source, target) in enumerate(pairs)
    ]
    for copy in copies:
        copy.start()
    return copies


def wait_all(copies):
    for copy in copies:
        copy.wait()


def fetch(weight):
    def body(source, target, sem):
        copy = pltpu.make_async_copy(source, target, sem)
        copy.start()
        copy.wait()

    return call(
        body,
        (in_hbm(weight),),
        [ANY],
        pltpu.VMEM(weight.shape, weight.dtype),
        data=2 * weight.size,
        limit=4,
        scratch=[pltpu.SemaphoreType.DMA],
    )


def chunk_of(size, most):
    while size % most:
        most //= 2
    return most


def exchanged(array, mask):
    count = lax.axis_size("dp")
    return lax.ppermute(array, "dp", [(i, i ^ mask) for i in range(count)])


def permuted(array, bit):
    return exchanged(array, 1 << bit)


def from_next_section(array):
    count = lax.axis_size("section")
    return lax.ppermute(array, "section", [(i + 1, i) for i in range(count - 1)])


def slot_tokens(ids, step, live):
    tokens = ids.shape[2]
    count = jnp.int32(0)
    held = [jnp.int32(-1)] * CAP
    for t in range(tokens):
        routed = ((ids[step, 0, t] == 0) | (ids[step, 1, t] == 0)) & live
        for c in range(CAP):
            held[c] = jnp.where(routed & (count == c), jnp.int32(t), held[c])
        count = count + routed.astype(jnp.int32)
    return held


def silu_parts(pre):
    sig = jax.nn.sigmoid(pre)
    return pre * sig, sig * (1.0 + pre * (1.0 - sig))


def softmax_rows(logits, experts):
    lane = iota(logits.shape, 1)
    expo = jnp.where(lane < experts, jnp.exp(logits), 0.0)
    return expo / jnp.sum(expo, axis=1, keepdims=True)


def first_minus(prob):
    lane = iota(prob.shape, 1)
    return jnp.where(lane == 0, 1.0, 0.0) - prob


def local(saved_inputs, carried, head_grad, routing, replica_counts, router, w_in, w_out):
    sections = lax.axis_size("section")
    n = lax.axis_size("dp")
    groups = n // QUARTERS
    width = head_grad.shape[1]
    tokens = head_grad.shape[0]
    part = w_in.shape[2]
    hidden = w_in.shape[3]
    half = hidden // 2
    experts = router.shape[2]
    rows = n * CAP
    router_t = router[0].T
    x_tok = saved_inputs[0].transpose(1, 0, 2)
    carried_tok = carried[0]
    ids = routing[0].transpose(0, 2, 1)
    last_section = sections - 1
    w1 = fetch(w_in[0, 0])

    def where_am_i():
        return lax.axis_index("section"), lax.axis_index("dp")

    def quarter_lanes():
        return pl.ds(pl.multiple_of(lax.rem(lax.axis_index("dp"), QUARTERS) * part, LANES), part)

    def half_lanes(core):
        return pl.ds(pl.multiple_of(core * half, LANES), half)

    def pick(held, value):
        row = iota((SLAB, value.shape[0]), 0)
        col = iota((SLAB, value.shape[0]), 1)
        chosen = jnp.zeros((SLAB, value.shape[0]), F32)
        for c in range(len(held)):
            chosen = chosen + jnp.where((row == c) & (col == held[c]), 1.0, 0.0)
        return dot(chosen.astype(BF), value)

    by_chip = n == 2 * QUARTERS

    def place_of(home):
        return jnp.bitwise_xor(home, lax.axis_index("dp")) if by_chip else home

    def send_quarters(slab_ref, slab, mine_ref, theirs_ref):
        slab_ref[...] = slab
        own = lax.rem(lax.axis_index("dp"), QUARTERS)
        for i in range(QUARTERS):
            at = pl.multiple_of(jnp.bitwise_xor(own, i) * part, LANES)
            ref = theirs_ref if i % 2 else mine_ref
            ref[i // 2] = slab_ref[:, pl.ds(at, part)].astype(BF)

    send_shapes = (sds((2, SLAB, part), BF), sds((2, SLAB, part), BF))
    slab_scratch = pltpu.VMEM((SLAB, width), F32)

    def spread(mine, theirs):
        if not by_chip:
            own = lax.rem(lax.axis_index("dp"), QUARTERS)
            quads = jnp.stack([mine[0], theirs[0], mine[1], theirs[1]])
            block = quads[jnp.bitwise_xor(jnp.arange(n) % QUARTERS, own)]
            return (lax.all_to_all(block, "dp", split_axis=0, concat_axis=0, tiled=True),)
        handed = permuted(theirs, 0)
        same = jnp.stack([mine[0], handed[0]])
        cross = jnp.stack([mine[1], handed[1]])
        return (same, exchanged(cross, 2), exchanged(same, 4), exchanged(cross, 6))

    def joined(refs):
        return jnp.concatenate([ref[...].reshape(-1, part) for ref in refs], axis=0)

    def dispatch_body(
        ids_hbm,
        counts_hbm,
        x_hbm,
        dy_hbm,
        mine_ref,
        theirs_ref,
        onward_ref,
        ids_ref,
        counts_ref,
        x_ref,
        dy_ref,
        slab_ref,
        sems,
    ):
        wait_all(
            copy_all(
                ((ids_hbm, ids_ref), (counts_hbm, counts_ref), (dy_hbm, dy_ref), (x_hbm, x_ref)),
                sems,
            )
        )
        section, dev = where_am_i()
        count = counts_ref[dev]
        held = [slot_tokens(ids_ref, step, step + section < count) for step in range(STEPS)]
        dy = dy_ref[...]
        slab = pick([-1] * (STEPS * CAP) + held[0], dy)
        row = iota((SLAB, width), 0)
        lane = lax.rem(iota((SLAB, width), 1), part)
        for step in range(STEPS):
            for c in range(CAP):
                value = x_ref[jnp.maximum(held[step][c], 0), step:step + 1, :].astype(F32)
                wanted = (row == step * CAP + c) & (held[step][c] >= 0)
                slab = jnp.where(wanted, jnp.broadcast_to(value, (SLAB, width)), slab)
        send_quarters(slab_ref, slab, mine_ref, theirs_ref)
        onward = pick(list(range(tokens)), dy)
        for c in range(CAP):
            code = (held[0][c] + 1).astype(F32)
            onward = jnp.where((row == tokens) & (lane == c), code, onward)
        onward_ref[...] = onward.astype(BF)

    mine, theirs, onward = call(
        dispatch_body,
        (in_hbm(ids), in_hbm(replica_counts), in_hbm(x_tok), in_hbm(carried_tok)),
        [ANY] * 4,
        (*send_shapes, sds((SLAB, width), BF)),
        data=4 * MIB,
        scratch=[
            pltpu.SMEM(ids.shape, jnp.int32),
            pltpu.SMEM(replica_counts.shape, jnp.int32),
            pltpu.VMEM(x_tok.shape, BF),
            pltpu.VMEM(carried_tok.shape, BF),
            slab_scratch,
            pltpu.SemaphoreType.DMA((4,)),
        ],
    )
    onward = from_next_section(onward)
    came = spread(mine, theirs)

    came, onward = lax.optimization_barrier((came, onward))

    wide = half + LANES

    def first_body(*refs):
        w1_ref, w2_hbm, router_hbm, xs_ref, ys_ref, keep_ref, send_ref, w2_ref, router_ref, sems = refs[
            len(came):
        ]
        core = lax.rem(lax.axis_index("dp"), 2)
        step = chunk_of(half, 512)
        router_copy = pltpu.make_async_copy(
            router_hbm.at[:, quarter_lanes()], router_ref, sems.at[0]
        )
        router_copy.start()
        chunks = [
            (ref, at, pl.multiple_of(which * half + at, LANES))
            for ref, which in ((send_ref, 1 - core), (keep_ref, core))
            for at in range(0, half, step)
        ]
        copies = copy_all(
            [(w2_hbm.at[pl.ds(lane, step)], w2_ref.at[pl.ds(lane, step)]) for _, _, lane in chunks],
            sems.at[pl.ds(1, len(chunks))],
        )
        flat = joined(refs[:len(came)])
        row = iota((STEPS * rows, n * SLAB), 0)
        col = iota((STEPS * rows, n * SLAB), 1)
        slot = row % rows
        want = place_of(slot // CAP) * SLAB + (row // rows) * CAP + slot % CAP
        xs = dot(one_hot(col == want), flat).astype(BF)
        row = iota((rows, n * SLAB), 0)
        col = iota((rows, n * SLAB), 1)
        ys = dot(one_hot(col == place_of(row // CAP) * SLAB + 2 * CAP + row % CAP), flat).astype(BF)
        xs_ref[...] = xs
        ys_ref[...] = ys
        router_copy.wait()
        logits = dot_hi(xs.astype(F32), router_ref[...], NT)
        logits = jnp.concatenate(
            [logits, jnp.zeros((STEPS * rows, LANES - experts), F32)], axis=1
        )
        zero = jnp.zeros((rows, LANES), F32)
        both = STEPS * rows
        for ref, at, lane in chunks:
            ref[0:both, at:at + step] = dot(xs, w1_ref[:, pl.ds(lane, step)])
        for ref in (send_ref, keep_ref):
            ref[0:both, half:wide] = logits
            ref[both:both + rows, half:wide] = zero
        for (ref, at, lane), copy in zip(chunks, copies):
            copy.wait()
            ref[both:both + rows, at:at + step] = dot(ys, w2_ref[pl.ds(lane, step), :], NT)

    xs, ys0, keep, send, w2, router_q = call(
        first_body,
        (*came, w1, in_hbm(w_out[0, 0]), in_hbm(router_t)),
        [VMEM] * (len(came) + 1) + [ANY] * 2,
        (
            sds((STEPS * rows, part), BF),
            sds((rows, part), BF),
            sds((3 * rows, wide), F32),
            sds((3 * rows, wide), F32),
            pltpu.VMEM((hidden, part), BF),
            sds((experts, part), F32),
        ),
        flops=2 * 3 * rows * part * hidden,
        data=2 * part * hidden * 2,
        scratch=[pltpu.SemaphoreType.DMA((1 + 2 * (half // chunk_of(half, 512)),))],
    )
    pair = keep + permuted(send, 0)
    mine0 = jnp.concatenate([pair[0:rows], pair[2 * rows:3 * rows]], axis=0)
    mine1 = pair[rows:2 * rows]
    other0 = permuted(mine0, 1)

    def base_body(
        ids_hbm,
        counts_hbm,
        onward_ref,
        head_hbm,
        mine_ref,
        theirs_ref,
        ids_ref,
        counts_ref,
        head_ref,
        slab_ref,
        sems,
    ):
        wait_all(
            copy_all(((ids_hbm, ids_ref), (counts_hbm, counts_ref), (head_hbm, head_ref)), sems)
        )
        section, dev = where_am_i()
        live = 1 + section < counts_ref[dev]
        last = section == last_section
        held = slot_tokens(ids_ref, 1, live)
        onward = onward_ref[...]
        slab = pick(held, jnp.where(last, head_ref[...], onward[0:tokens]))
        row = iota((SLAB, width), 0)
        code = jnp.broadcast_to(onward[tokens:tokens + 1].astype(F32), (SLAB, width))
        for c in range(CAP):
            same = (held[c] >= 0) & (code == (held[c] + 1).astype(F32))
            slab = jnp.where((row == CAP + c) & same, 1.0, slab)
        send_quarters(slab_ref, slab, mine_ref, theirs_ref)

    base_sent = call(
        base_body,
        (in_hbm(ids), in_hbm(replica_counts), onward, in_hbm(head_grad)),
        [ANY, ANY, VMEM, ANY],
        send_shapes,
        data=4 * MIB,
        scratch=[
            pltpu.SMEM(ids.shape, jnp.int32),
            pltpu.SMEM(replica_counts.shape, jnp.int32),
            pltpu.VMEM(head_grad.shape, BF),
            slab_scratch,
            pltpu.SemaphoreType.DMA((3,)),
        ],
    )
    base = spread(*base_sent)
    other0, base = lax.optimization_barrier((other0, base))

    def gated(pre, upper, gate):
        act, slope = silu_parts(pre)
        dpre = (gate * upper * slope).astype(BF)
        block = jnp.sum(act * upper, axis=1, keepdims=True)
        return act, dpre, block

    def split_sum(block):
        high = block.astype(BF)
        low = (block - high.astype(F32)).astype(BF)
        lane = iota((rows, LANES), 1)
        zero = jnp.zeros((rows, LANES), BF)
        return jnp.where(lane == 0, high, jnp.where(lane == 1, low, zero))

    def gate_of(prob):
        return prob[:, 0:1].astype(BF).astype(F32)

    def act0_body(a_ref, b_ref, out_ref, prob_ref, block_ref):
        prob = softmax_rows(a_ref[0:rows, half:wide] + b_ref[0:rows, half:wide], experts)
        gate = gate_of(prob)
        pre = a_ref[0:rows, 0:half] + b_ref[0:rows, 0:half]
        upper = a_ref[rows:2 * rows, 0:half] + b_ref[rows:2 * rows, 0:half]
        act, dpre, block = gated(pre, upper, gate)
        out_ref[:, 0:half] = dpre
        out_ref[:, half:wide] = split_sum(block)
        out_ref[:, wide:wide + half] = (gate * act).astype(BF)
        prob_ref[...] = prob
        block_ref[...] = jnp.broadcast_to(block, (rows, LANES))

    hid0, prob0, block0 = call(
        act0_body,
        (mine0, other0),
        [VMEM] * 2,
        (sds((rows, wide + half), BF), sds((rows, LANES), F32), sds((rows, LANES), F32)),
    )
    hid0_pair = permuted(hid0, 0)

    def block_sum(block, pair_ref):
        extra = pair_ref[:, half:half + 1].astype(F32) + pair_ref[:, half + 1:half + 2].astype(F32)
        return (block[:, 0:1] + extra).astype(BF)

    def in_order(own, pair, core):
        return (
            jnp.where(core == 0, own, pair),
            jnp.where(core == 0, pair, own),
        )

    def dx_of(own_ref, pair_ref, w1_ref, core):
        low, high = in_order(own_ref[:, 0:half], pair_ref[:, 0:half], core)
        step = chunk_of(part, 256)
        pieces = []
        for at in range(0, part, step):
            pieces.append(
                dot(low, w1_ref[at:at + step, 0:half], NT)
                + dot(high, w1_ref[at:at + step, half:hidden], NT)
            )
        return jnp.concatenate(pieces, axis=1)

    def dx0_body(own_ref, pair_ref, block_ref, w1_ref, out_ref):
        core = lax.rem(lax.axis_index("dp"), 2)
        out_ref[:, 0:part] = dx_of(own_ref, pair_ref, w1_ref, core).astype(BF)
        dgate = block_sum(block_ref[...], pair_ref)
        lane = iota((rows, LANES), 1)
        out_ref[:, part:part + LANES] = jnp.where(
            lane == 0, jnp.broadcast_to(dgate, (rows, LANES)), jnp.zeros((rows, LANES), BF)
        )

    dx0 = call(
        dx0_body,
        (hid0, hid0_pair, block0, w1),
        [VMEM] * 4,
        sds((rows, part + LANES), BF),
        flops=2 * rows * part * hidden,
        data=2 * part * hidden,
    )
    total0, bit = dx0, 2
    while (1 << (bit + 1)) < n:
        total0 = total0.astype(F32) + permuted(total0, bit).astype(F32)
        bit += 1
    other_total0 = permuted(total0, bit) if groups > 1 else jnp.zeros_like(total0)

    def sum0_body(a_ref, b_ref, prob_ref, router_ref, out_ref, dlog_ref):
        total = a_ref[...].astype(F32) + b_ref[...].astype(F32)
        prob = prob_ref[...]
        dlog = total[:, part:part + 1] * prob[:, 0:1] * first_minus(prob)
        dlog_ref[...] = dlog
        back = dot_hi(dlog[:, 0:experts], router_ref[...])
        out_ref[...] = (total[:, 0:part] + back).astype(BF)

    dxs0, dlog0 = call(
        sum0_body,
        (total0, other_total0, prob0, router_q),
        [VMEM] * 4,
        (sds((rows, part), BF), sds((rows, LANES), F32)),
    )
    dxs_next = from_next_section(dxs0)
    other1 = permuted(mine1, 1)
    dxs_next, other1 = lax.optimization_barrier((dxs_next, other1))


    def up1_body(*refs):
        dxs_ref, w2_ref, ys_ref, keep_ref, send_ref = refs[len(base):]
        core = lax.rem(lax.axis_index("dp"), 2)
        flat = joined(refs[:len(base)])
        row = iota((rows, n * SLAB), 0)
        col = iota((rows, n * SLAB), 1)
        want = place_of(row // CAP) * SLAB + row % CAP
        value = dot(one_hot(col == want), flat)
        match = dot(one_hot(col == want + CAP), flat[:, 0:LANES])
        row = iota((rows, rows), 0)
        col = iota((rows, rows), 1)
        place = jnp.zeros((rows, rows), F32)
        for b in range(CAP):
            place = place + jnp.where(
                (row // CAP == col // CAP) & (col % CAP == b), match[:, b:b + 1], 0.0
            )
        ys = (value + dot(place.astype(BF), dxs_ref[...])).astype(BF)
        ys_ref[...] = ys
        step = chunk_of(half, 512)
        for ref, which in ((send_ref, 1 - core), (keep_ref, core)):
            for at in range(0, half, step):
                lanes = pl.ds(pl.multiple_of(which * half + at, LANES), step)
                ref[:, at:at + step] = dot(ys, w2_ref[lanes, :], NT)

    ys1, keep1, send1 = call(
        up1_body,
        (*base, dxs_next, w2),
        [VMEM] * (len(base) + 2),
        (sds((rows, part), BF), sds((rows, half), F32), sds((rows, half), F32)),
        flops=2 * rows * part * hidden,
        data=2 * part * hidden,
    )
    up1 = keep1 + permuted(send1, 0)
    other_up1 = permuted(up1, 1)

    def act1_body(a_ref, b_ref, out_ref, prob_ref):
        prob = softmax_rows(a_ref[:, half:wide] + b_ref[:, half:wide], experts)
        act, _ = silu_parts(a_ref[:, 0:half] + b_ref[:, 0:half])
        out_ref[...] = (gate_of(prob) * act).astype(BF)
        prob_ref[...] = prob

    scaled1, prob1 = call(
        act1_body,
        (mine1, other1),
        [VMEM] * 2,
        (sds((rows, half), BF), sds((rows, LANES), F32)),
    )
    scaled1_pair = permuted(scaled1, 0)

    both = STEPS * rows

    def outer(body, args, height, across, flops):
        return call(
            body,
            args,
            [VMEM] * len(args),
            sds((height, across), BF),
            flops=flops,
            data=2 * height * across,
            limit=22,
            out_specs=ANY,
            scratch=[
                pltpu.VMEM((height, across), BF),
                pltpu.SemaphoreType.DMA((SLAB,)),
            ],
        )

    def write_out(a, b, out_ref, held_ref, sems):
        height = held_ref.shape[0]
        step = height // SLAB
        copies = []
        for i in range(SLAB):
            at = pl.ds(i * step, step)
            held_ref[i * step:(i + 1) * step, :] = dot(
                a[:, i * step:(i + 1) * step], b, TN
            ).astype(BF)
            copy = pltpu.make_async_copy(held_ref.at[at], out_ref.at[at], sems.at[i])
            copy.start()
            copies.append(copy)
        for copy in copies:
            copy.wait()

    def grad_out_body(own0, pair0, own1, pair1, ys0_ref, ys1_ref, out_ref, held_ref, sems):
        core = lax.rem(lax.axis_index("dp"), 2)
        a0, b0 = in_order(own0[:, wide:wide + half], pair0[:, wide:wide + half], core)
        a1, b1 = in_order(own1[...], pair1[...], core)
        scaled = jnp.concatenate(
            [jnp.concatenate([a0, b0], axis=1), jnp.concatenate([a1, b1], axis=1)], axis=0
        )
        ys = jnp.concatenate([ys0_ref[...], ys1_ref[...]], axis=0)
        write_out(scaled, ys, out_ref, held_ref, sems)

    grad_out = outer(
        grad_out_body,
        (hid0, hid0_pair, scaled1, scaled1_pair, ys0, ys1),
        hidden,
        part,
        2 * both * part * hidden,
    )

    other_up1, grad_out = lax.optimization_barrier((other_up1, grad_out))

    def act2_body(a_ref, b_ref, up_ref, other_ref, prob_ref, out_ref, block_ref):
        pre = a_ref[:, 0:half] + b_ref[:, 0:half]
        upper = up_ref[...] + other_ref[...]
        _, dpre, block = gated(pre, upper, gate_of(prob_ref[...]))
        out_ref[:, 0:half] = dpre
        out_ref[:, half:wide] = split_sum(block)
        block_ref[...] = jnp.broadcast_to(block, (rows, LANES))

    hid1, block1 = call(
        act2_body,
        (mine1, other1, up1, other_up1, prob1),
        [VMEM] * 5,
        (sds((rows, wide), BF), sds((rows, LANES), F32)),
    )
    hid1_pair = permuted(hid1, 0)

    back_rows = 2 * SLAB

    def dx1_body(
        own_ref, pair_ref, block_ref, prob_ref, dlog0_ref, xs_ref, dxs0_ref, next_ref, router_ref, w1_ref, out_ref
    ):
        dev = lax.axis_index("dp")
        core = lax.rem(dev, 2)
        group = dev // QUARTERS
        dx = dx_of(own_ref, pair_ref, w1_ref, core)
        prob = prob_ref[...]
        dgate = block_sum(block_ref[...], pair_ref).astype(F32)
        dlog = dgate * prob[:, 0:1] * first_minus(prob)
        dx = (dx + dot_hi(dlog[:, 0:experts], router_ref[...])).astype(BF)
        aux = jnp.where(group == 0, dxs0_ref[...], next_ref[...])
        dlogs = jnp.concatenate(
            [jnp.where(group == 0, dlog0_ref[...], 0.0), dlog], axis=0
        )
        grad = dot_hi(dlogs, xs_ref[...].astype(F32), TN)[0:experts, :].astype(BF)
        source = jnp.concatenate([dx, aux, grad], axis=0)
        count = 2 * rows + experts
        row = iota((n * back_rows, count), 0)
        col = iota((n * back_rows, count), 1)
        home = row // back_rows
        kind = row % back_rows
        want = jnp.where(
            kind < 2 * CAP,
            (kind // CAP) * rows + home * CAP + kind % CAP,
            jnp.where(kind >= SLAB, 2 * rows + kind - SLAB, -1),
        )
        out_ref[...] = dot(one_hot(col == want), source).astype(BF).reshape(n, back_rows, part)

    back_sent = call(
        dx1_body,
        (hid1, hid1_pair, block1, prob1, dlog0, xs, dxs0, dxs_next, router_q, w1),
        [VMEM] * 10,
        sds((n, back_rows, part), BF),
        flops=2 * rows * part * hidden,
        data=2 * part * hidden,
        limit=16,
    )
    back = lax.all_to_all(back_sent, "dp", split_axis=0, concat_axis=0, tiled=True)

    def grad_in_body(own0, pair0, own1, pair1, xs_ref, out_ref, held_ref, sems):
        core = lax.rem(lax.axis_index("dp"), 2)
        a0, b0 = in_order(own0[:, 0:half], pair0[:, 0:half], core)
        a1, b1 = in_order(own1[:, 0:half], pair1[:, 0:half], core)
        dpre = jnp.concatenate(
            [jnp.concatenate([a0, b0], axis=1), jnp.concatenate([a1, b1], axis=1)], axis=0
        )
        write_out(xs_ref[...], dpre, out_ref, held_ref, sems)

    grad_in = outer(
        grad_in_body,
        (hid0, hid0_pair, hid1, hid1_pair, xs),
        part,
        hidden,
        2 * both * part * hidden,
    )

    def final_body(
        ids_ref, counts_ref, back_ref, dy_ref, onward_ref, head_ref, out_ref, router_out_ref
    ):
        section, dev = where_am_i()
        count = counts_ref[dev]
        last = section == last_section
        live0 = section < count
        live1 = 1 + section < count
        held0 = slot_tokens(ids_ref, 0, live0)
        held1 = slot_tokens(ids_ref, 1, live1)
        onward = onward_ref[...].astype(F32)
        before = [onward[tokens:tokens + 1, c:c + 1] - 1.0 for c in range(CAP)]
        wide_dy = jnp.where(live0, dy_ref[...].astype(F32), 0.0)
        dy1 = jnp.where(last, head_ref[...].astype(F32), onward[0:tokens])
        wide_dy1 = jnp.where(live1, dy1, 0.0)

        def put(held, at, value):
            row = iota((tokens, 2 * SLAB), 0)
            col = iota((tokens, 2 * SLAB), 1)
            place = jnp.zeros((tokens, 2 * SLAB), F32)
            for c in range(CAP):
                mine = row.astype(F32) == held[c].astype(F32)
                place = place + jnp.where(mine & (col == at + c), 1.0, 0.0)
            return dot(place.astype(BF), value)

        for q in range(QUARTERS):
            lanes = slice(q * part, (q + 1) * part)
            blocks = [back_ref[g * QUARTERS + q] for g in range(groups)]
            grad = blocks[0][SLAB:SLAB + experts].astype(F32)
            for block in blocks[1:]:
                grad = grad + block[SLAB:SLAB + experts].astype(F32)
            router_out_ref[:, lanes] = grad
            out0 = wide_dy[:, lanes] + put(held0, CAP, blocks[0])
            out1 = wide_dy1[:, lanes]
            if groups > 1:
                out1 = out1 + put(before, CAP, blocks[1])
            out1 = out1.astype(BF).astype(F32)
            for block in blocks:
                out1 = out1 + put(held1, 0, block)
            out0 = out0.astype(BF)
            out1 = out1.astype(BF)
            for t in range(tokens):
                out_ref[t, 0:1, lanes] = out0[t:t + 1]
                out_ref[t, 1:2, lanes] = out1[t:t + 1]

    grads, router_grad = call(
        final_body,
        (ids, replica_counts, back, carried_tok, onward, head_grad),
        [SMEM, SMEM, VMEM, VMEM, VMEM, VMEM],
        (sds((tokens, STEPS, width), BF), sds((experts, width), F32)),
        limit=24,
    )
    input_grad = grads.transpose(1, 0, 2)[:, None]
    return (input_grad, grad_in[None, None], grad_out[None, None], router_grad.T[None])


def solution(mesh):
    in_specs = (
        P("section", None, "dp", None),
        P("section", "dp", None),
        P("dp", None),
        P("section", None, "dp", None),
        P(),
        P("section", None, None),
        P("section", "dp", None, None),
        P("section", "dp", None, None),
    )
    out_specs = (
        P(None, "section", "dp", None),
        P("section", "dp", None, None),
        P("section", "dp", None, None),
        P("section", None, None),
    )
    return jax.shard_map(local, mesh=mesh, in_specs=in_specs, out_specs=out_specs, check_vma=False)
```

```python
import functools

import jax
import jax.numpy as jnp
from jax import lax
from jax.experimental import pallas as pl
from jax.experimental.pallas import tpu as pltpu
from jax.sharding import PartitionSpec as P

STEPS = 2
CAP = 2
QUARTERS = 4
LANES = 128
SLAB = 8
BF = jnp.bfloat16
F32 = jnp.float32
MIB = 1 << 20

NN = (((1,), (0,)), ((), ()))
NT = (((1,), (1,)), ((), ()))
TN = (((0,), (0,)), ((), ()))

VMEM = pl.BlockSpec(memory_space=pltpu.VMEM)
SMEM = pl.BlockSpec(memory_space=pltpu.SMEM)
ANY = pl.BlockSpec(memory_space=pl.ANY)


def dot(a, b, dims=NN):
    return lax.dot_general(a, b, dims, preferred_element_type=F32)


def split3(a):
    high = a.astype(BF)
    rest = a - high.astype(F32)
    mid = rest.astype(BF)
    return high, mid, (rest - mid.astype(F32)).astype(BF)


def dot_split(a, b, dims):
    at_a, at_b = dims[0][0][0], dims[0][1][0]
    a0, a1, a2 = split3(a)
    b0, b1, b2 = split3(b)
    return dot(
        jnp.concatenate([a0, a0, a1, a0, a1, a2], axis=at_a),
        jnp.concatenate([b0, b1, b0, b2, b1, b0], axis=at_b),
        dims,
    )


def iota(shape, dim):
    return lax.broadcasted_iota(jnp.int32, shape, dim)


def one_hot(cond):
    return jnp.where(cond, 1.0, 0.0).astype(BF)


def sds(shape, dtype):
    return jax.ShapeDtypeStruct(shape, dtype)


def call(body, args, specs, outs, flops=0, data=0, limit=12, scratch=(), out_specs=None, aliases=None):
    many = isinstance(outs, tuple)
    if out_specs is None:
        out_specs = tuple(VMEM for _ in outs) if many else VMEM
    return pl.pallas_call(
        body,
        in_specs=specs,
        out_specs=out_specs,
        out_shape=outs,
        scratch_shapes=scratch,
        input_output_aliases=aliases or {},
        cost_estimate=pl.CostEstimate(flops=flops, bytes_accessed=data, transcendentals=0),
        compiler_params=pltpu.CompilerParams(vmem_limit_bytes=limit * MIB),
    )(*args)


def in_hbm(array):
    return pltpu.with_memory_space_constraint(array, pltpu.HBM)


def copy_all(pairs, sems):
    copies = [
        pltpu.make_async_copy(source, target, sems.at[i])
        for i, (source, target) in enumerate(pairs)
    ]
    for copy in copies:
        copy.start()
    return copies


def wait_all(copies):
    for copy in copies:
        copy.wait()


def fetch(weight):
    def body(source, target, sem):
        copy = pltpu.make_async_copy(source, target, sem)
        copy.start()
        copy.wait()

    return call(
        body,
        (in_hbm(weight),),
        [ANY],
        pltpu.VMEM(weight.shape, weight.dtype),
        data=2 * weight.size,
        limit=4,
        scratch=[pltpu.SemaphoreType.DMA],
    )


def chunk_of(size, most):
    while size % most:
        most //= 2
    return most


def exchanged(array, mask):
    count = lax.axis_size("dp")
    return lax.ppermute(array, "dp", [(i, i ^ mask) for i in range(count)])


def permuted(array, bit):
    return exchanged(array, 1 << bit)


def from_next_section(array, mask=0):
    count, devices = lax.axis_size("section"), lax.axis_size("dp")
    pairs = [
        (d * count + i + 1, (d ^ mask) * count + i) for d in range(devices) for i in range(count - 1)
    ]
    return lax.ppermute(array, ("dp", "section"), pairs)


def slot_tokens(ids, step, live):
    tokens = ids.shape[2]
    count = jnp.int32(0)
    held = [jnp.int32(-1)] * CAP
    for t in range(tokens):
        routed = ((ids[step, 0, t] == 0) | (ids[step, 1, t] == 0)) & live
        for c in range(CAP):
            held[c] = jnp.where(routed & (count == c), jnp.int32(t), held[c])
        count = count + routed.astype(jnp.int32)
    return held


def silu_parts(pre):
    sig = jax.nn.sigmoid(pre)
    return pre * sig, sig * (1.0 + pre * (1.0 - sig))


def softmax_rows(logits):
    expo = jnp.exp(logits)
    prob = expo / jnp.sum(expo, axis=1, keepdims=True)
    rows, experts = logits.shape
    return jnp.concatenate([prob, jnp.zeros((rows, LANES - experts), F32)], axis=1)


def first_minus(prob):
    lane = iota(prob.shape, 1)
    return jnp.where(lane == 0, 1.0, 0.0) - prob


def local(saved_inputs, carried, head_grad, routing, replica_counts, router, w_in, w_out):
    sections = lax.axis_size("section")
    n = lax.axis_size("dp")
    groups = n // QUARTERS
    width = head_grad.shape[1]
    tokens = head_grad.shape[0]
    part = w_in.shape[2]
    hidden = w_in.shape[3]
    half = hidden // 2
    experts = router.shape[2]
    rows = n * CAP
    router_t = router[0].T
    x_tok = saved_inputs[0].transpose(1, 0, 2)
    carried_tok = carried[0]
    ids = routing[0].transpose(0, 2, 1)
    last_section = sections - 1
    w1 = fetch(w_in[0, 0])

    def where_am_i():
        return lax.axis_index("section"), lax.axis_index("dp")

    def quarter_lanes():
        return pl.ds(pl.multiple_of(lax.rem(lax.axis_index("dp"), QUARTERS) * part, LANES), part)

    def half_lanes(core):
        return pl.ds(pl.multiple_of(core * half, LANES), half)

    def pick(held, value):
        row = iota((SLAB, value.shape[0]), 0)
        col = iota((SLAB, value.shape[0]), 1)
        chosen = jnp.zeros((SLAB, value.shape[0]), F32)
        for c in range(len(held)):
            chosen = chosen + jnp.where((row == c) & (col == held[c]), 1.0, 0.0)
        return dot(chosen.astype(BF), value)

    by_chip = n == 2 * QUARTERS

    def place_of(home):
        return jnp.bitwise_xor(home, lax.axis_index("dp")) if by_chip else home

    def send_quarters(slab_ref, slab, mine_ref, theirs_ref):
        slab_ref[...] = slab
        own = lax.rem(lax.axis_index("dp"), QUARTERS)
        for i in range(QUARTERS):
            at = pl.multiple_of(jnp.bitwise_xor(own, i) * part, LANES)
            ref = theirs_ref if i % 2 else mine_ref
            ref[i // 2] = slab_ref[:, pl.ds(at, part)].astype(BF)

    send_shapes = (sds((2, SLAB, part), BF), sds((2, SLAB, part), BF))
    slab_scratch = pltpu.VMEM((SLAB, width), F32)

    def spread_whole(mine, theirs):
        own = lax.rem(lax.axis_index("dp"), QUARTERS)
        quads = jnp.stack([mine[0], theirs[0], mine[1], theirs[1]])
        block = quads[jnp.bitwise_xor(jnp.arange(n) % QUARTERS, own)]
        return (lax.all_to_all(block, "dp", split_axis=0, concat_axis=0, tiled=True),)

    def spread_in_chip(mine, theirs):
        handed = permuted(theirs, 0)
        return jnp.stack([mine[0], handed[0]]), jnp.stack([mine[1], handed[1]])

    def joined(refs):
        return jnp.concatenate([ref[...].reshape(-1, part) for ref in refs], axis=0)

    def dispatch_body(
        ids_hbm,
        counts_hbm,
        x_hbm,
        dy_hbm,
        mine_ref,
        theirs_ref,
        onward_ref,
        ids_ref,
        counts_ref,
        x_ref,
        dy_ref,
        slab_ref,
        sems,
    ):
        wait_all(
            copy_all(
                ((ids_hbm, ids_ref), (counts_hbm, counts_ref), (dy_hbm, dy_ref), (x_hbm, x_ref)),
                sems,
            )
        )
        section, dev = where_am_i()
        count = counts_ref[dev]
        held = [slot_tokens(ids_ref, step, step + section < count) for step in range(STEPS)]
        dy = dy_ref[...]
        slab = pick([-1] * (STEPS * CAP) + held[0], dy)
        row = iota((SLAB, width), 0)
        lane = lax.rem(iota((SLAB, width), 1), part)
        for step in range(STEPS):
            for c in range(CAP):
                value = x_ref[jnp.maximum(held[step][c], 0), step:step + 1, :].astype(F32)
                wanted = (row == step * CAP + c) & (held[step][c] >= 0)
                slab = jnp.where(wanted, jnp.broadcast_to(value, (SLAB, width)), slab)
        send_quarters(slab_ref, slab, mine_ref, theirs_ref)
        onward = pick(list(range(tokens)), dy)
        for c in range(CAP):
            code = (held[0][c] + 1).astype(F32)
            onward = jnp.where((row == tokens) & (lane == c), code, onward)
        onward_ref[...] = onward.astype(BF)

    mine, theirs, onward = call(
        dispatch_body,
        (in_hbm(ids), in_hbm(replica_counts), in_hbm(x_tok), in_hbm(carried_tok)),
        [ANY] * 4,
        (*send_shapes, sds((SLAB, width), BF)),
        data=4 * MIB,
        scratch=[
            pltpu.SMEM(ids.shape, jnp.int32),
            pltpu.SMEM(replica_counts.shape, jnp.int32),
            pltpu.VMEM(x_tok.shape, BF),
            pltpu.VMEM(carried_tok.shape, BF),
            slab_scratch,
            pltpu.SemaphoreType.DMA((4,)),
        ],
    )
    onward = from_next_section(onward)
    if by_chip:
        same, cross = spread_in_chip(mine, theirs)
        came = (same, exchanged(cross, 2), exchanged(same, 4), exchanged(cross, 6))
    else:
        came = spread_whole(mine, theirs)
    came, onward = lax.optimization_barrier((came, onward))

    wide = half + LANES

    def first_body(*refs):
        w1_ref, w2_hbm, router_hbm, xs_ref, ys_ref, keep_ref, send_ref, w2_ref, router_ref, sems = refs[
            len(came):
        ]
        core = lax.rem(lax.axis_index("dp"), 2)
        step = chunk_of(half, 512)
        router_copy = pltpu.make_async_copy(
            router_hbm.at[:, quarter_lanes()], router_ref, sems.at[0]
        )
        router_copy.start()
        chunks = [
            (ref, at, pl.multiple_of(which * half + at, LANES))
            for ref, which in ((send_ref, 1 - core), (keep_ref, core))
            for at in range(0, half, step)
        ]
        copies = copy_all(
            [(w2_hbm.at[pl.ds(lane, step)], w2_ref.at[pl.ds(lane, step)]) for _, _, lane in chunks],
            sems.at[pl.ds(1, len(chunks))],
        )

        @pl.when(lax.axis_index("dp") >= 0)
        def _():
            flat = joined(refs[:len(came)])
            row = iota((STEPS * rows, n * SLAB), 0)
            col = iota((STEPS * rows, n * SLAB), 1)
            slot = row % rows
            want = place_of(slot // CAP) * SLAB + (row // rows) * CAP + slot % CAP
            xs = dot(one_hot(col == want), flat).astype(BF)
            row = iota((rows, n * SLAB), 0)
            col = iota((rows, n * SLAB), 1)
            ys = dot(one_hot(col == place_of(row // CAP) * SLAB + 2 * CAP + row % CAP), flat).astype(BF)
            xs_ref[...] = xs
            ys_ref[...] = ys
            router_copy.wait()
            parts = jnp.concatenate(
                [
                    jnp.concatenate([p, jnp.zeros((LANES - experts, part), BF)], axis=0)
                    for p in split3(router_ref[...])
                ],
                axis=0,
            )
            logits = dot(xs, parts, NT)
            logits = logits[:, 0:LANES] + logits[:, LANES:2 * LANES] + logits[:, 2 * LANES:3 * LANES]
            zero = jnp.zeros((rows, LANES), F32)
            both = STEPS * rows
            for ref, at, lane in chunks:
                ref[0:both, at:at + step] = dot(xs, w1_ref[:, pl.ds(lane, step)])
            for ref in (send_ref, keep_ref):
                ref[0:both, half:wide] = logits
                ref[both:both + rows, half:wide] = zero
            for (ref, at, lane), copy in zip(chunks, copies):
                copy.wait()
                ref[both:both + rows, at:at + step] = dot(ys, w2_ref[pl.ds(lane, step), :], NT)

    xs, ys0, keep, send, w2, router_q = call(
        first_body,
        (*came, w1, in_hbm(w_out[0, 0]), in_hbm(router_t)),
        [VMEM] * (len(came) + 1) + [ANY] * 2,
        (
            sds((STEPS * rows, part), BF),
            sds((rows, part), BF),
            sds((3 * rows, wide), F32),
            sds((3 * rows, wide), F32),
            pltpu.VMEM((hidden, part), BF),
            sds((experts, part), F32),
        ),
        flops=2 * 3 * rows * part * hidden,
        data=2 * part * hidden * 2,
        scratch=[pltpu.SemaphoreType.DMA((1 + 2 * (half // chunk_of(half, 512)),))],
    )
    send, onward = lax.optimization_barrier((send, onward))
    send_other = permuted(send, 0)

    def base_body(
        ids_hbm,
        counts_hbm,
        onward_ref,
        head_hbm,
        mine_ref,
        theirs_ref,
        ids_ref,
        counts_ref,
        head_ref,
        slab_ref,
        sems,
    ):
        wait_all(
            copy_all(((ids_hbm, ids_ref), (counts_hbm, counts_ref), (head_hbm, head_ref)), sems)
        )
        section, dev = where_am_i()
        live = 1 + section < counts_ref[dev]
        last = section == last_section
        held = slot_tokens(ids_ref, 1, live)
        onward = onward_ref[...]
        slab = pick(held, jnp.where(last, head_ref[...], onward[0:tokens]))
        row = iota((SLAB, width), 0)
        code = jnp.broadcast_to(onward[tokens:tokens + 1].astype(F32), (SLAB, width))
        for c in range(CAP):
            same = (held[c] >= 0) & (code == (held[c] + 1).astype(F32))
            slab = jnp.where((row == CAP + c) & same, 1.0, slab)
        send_quarters(slab_ref, slab, mine_ref, theirs_ref)

    base_sent = call(
        base_body,
        (in_hbm(ids), in_hbm(replica_counts), onward, in_hbm(head_grad)),
        [ANY, ANY, VMEM, ANY],
        send_shapes,
        data=4 * MIB,
        scratch=[
            pltpu.SMEM(ids.shape, jnp.int32),
            pltpu.SMEM(replica_counts.shape, jnp.int32),
            pltpu.VMEM(head_grad.shape, BF),
            slab_scratch,
            pltpu.SemaphoreType.DMA((3,)),
        ],
    )
    send_other, base_sent = lax.optimization_barrier((send_other, base_sent))

    def pair_body(keep_ref, other_ref, mine0_ref, mine1_ref, narrow0_ref, narrow1_ref):
        both = STEPS * rows
        for at, ref, narrow, to in (
            (0, mine0_ref, narrow0_ref, 0),
            (both, mine0_ref, narrow0_ref, rows),
            (rows, mine1_ref, narrow1_ref, 0),
        ):
            total = keep_ref[at:at + rows, :] + other_ref[at:at + rows, :]
            ref[to:to + rows, :] = total
            narrow[to:to + rows, 0:half] = total[:, 0:half].astype(BF)
            pieces = split3(total[:, half:half + experts])
            spare = jnp.zeros((rows, LANES - 3 * experts), BF)
            narrow[to:to + rows, half:wide] = jnp.concatenate([*pieces, spare], axis=1)

    mine0, mine1, narrow0, narrow1 = call(
        pair_body,
        (keep, send_other),
        [VMEM] * 2,
        (
            sds((2 * rows, wide), F32),
            sds((rows, wide), F32),
            sds((2 * rows, wide), BF),
            sds((rows, wide), BF),
        ),
    )
    other0 = permuted(narrow0, 1)

    used = 2 * CAP
    if by_chip:
        base_handed = permuted(base_sent[1], 0)

        def join_body(mine_ref, handed_ref, same_ref, cross_ref):
            for i, ref in enumerate((same_ref, cross_ref)):
                ref[...] = jnp.concatenate([mine_ref[i, 0:used], handed_ref[i, 0:used]], axis=0)

        base_same, base_cross = call(
            join_body,
            (base_sent[0], base_handed),
            [VMEM] * 2,
            (sds((2 * used, part), BF), sds((2 * used, part), BF)),
        )
        base_beside = exchanged(base_cross, 2)
        other0, base_beside = lax.optimization_barrier((other0, base_beside))

        def four_body(same_ref, beside_ref, out_ref):
            out_ref[...] = jnp.concatenate([same_ref[...], beside_ref[...]], axis=0)

        base_four = call(four_body, (base_same, base_beside), [VMEM] * 2, sds((4 * used, part), BF))
    else:
        base_whole = spread_whole(*base_sent)[0][:, 0:used]

    def all_logits(own, other):
        at = half + experts
        pieces = [other[:, half + i * experts:at + i * experts].astype(F32) for i in range(3)]
        return own[:, half:at] + (pieces[0] + pieces[1] + pieces[2])

    def gated(pre, upper, gate):
        act, slope = silu_parts(pre)
        dpre = (gate * upper * slope).astype(BF)
        block = jnp.sum(act * upper, axis=1, keepdims=True)
        return act, dpre, block

    def split_sum(block):
        high = block.astype(BF)
        low = (block - high.astype(F32)).astype(BF)
        lane = iota((rows, LANES), 1)
        zero = jnp.zeros((rows, LANES), BF)
        return jnp.where(lane == 0, high, jnp.where(lane == 1, low, zero))

    def gate_of(prob):
        return prob[:, 0:1].astype(BF).astype(F32)

    def act0_body(a_ref, b_ref, out_ref, prob_ref, block_ref):
        total = a_ref[:, 0:half] + b_ref[:, 0:half].astype(F32)
        prob = softmax_rows(all_logits(a_ref[0:rows, :], b_ref[0:rows, :]))
        gate = gate_of(prob)
        pre = total[0:rows]
        upper = total[rows:2 * rows]
        act, dpre, block = gated(pre, upper, gate)
        out_ref[:, 0:half] = dpre
        out_ref[:, half:wide] = split_sum(block)
        out_ref[:, wide:wide + half] = (gate * act).astype(BF)
        prob_ref[...] = prob
        block_ref[...] = jnp.broadcast_to(block, (rows, LANES))

    hid0, prob0, block0 = call(
        act0_body,
        (mine0, other0),
        [VMEM] * 2,
        (sds((rows, wide + half), BF), sds((rows, LANES), F32), sds((rows, LANES), F32)),
    )
    hid0_pair = permuted(hid0, 0)

    def block_sum(block, pair_ref):
        extra = pair_ref[:, half:half + 1].astype(F32) + pair_ref[:, half + 1:half + 2].astype(F32)
        return (block[:, 0:1] + extra).astype(BF)

    def in_order(own, pair, core):
        return (
            jnp.where(core == 0, own, pair),
            jnp.where(core == 0, pair, own),
        )

    def dx_of(own_ref, pair_ref, w1_ref, core):
        low, high = in_order(own_ref[:, 0:half], pair_ref[:, 0:half], core)
        step = chunk_of(part, 256)
        pieces = []
        for at in range(0, part, step):
            pieces.append(
                dot(low, w1_ref[at:at + step, 0:half], NT)
                + dot(high, w1_ref[at:at + step, half:hidden], NT)
            )
        return jnp.concatenate(pieces, axis=1)

    def routed_back(dx, block_ref, pair_ref, prob, router_ref):
        dgate = block_sum(block_ref[...], pair_ref).astype(F32)
        dlog = dgate * prob[:, 0:1] * first_minus(prob)
        return (dx + dot_split(dlog[:, 0:experts], router_ref[...], NN)).astype(BF), dlog

    def dx0_body(own_ref, pair_ref, block_ref, prob_ref, router_ref, w1_ref, out_ref, dlog_ref):
        core = lax.rem(lax.axis_index("dp"), 2)
        dx = dx_of(own_ref, pair_ref, w1_ref, core)
        out_ref[...], dlog_ref[...] = routed_back(dx, block_ref, pair_ref, prob_ref[...], router_ref)

    dx0, dlog0 = call(
        dx0_body,
        (hid0, hid0_pair, block0, prob0, router_q, w1),
        [VMEM] * 6,
        (sds((rows, part), BF), sds((rows, LANES), F32)),
        flops=2 * rows * part * hidden,
        data=2 * part * hidden,
    )
    if by_chip:
        dx0, narrow1, base_four = lax.optimization_barrier((dx0, narrow1, base_four))
        base = (base_four, exchanged(base_four, 4))
    else:
        base = (base_whole.reshape(n * used, part),)
    cut = half // 2
    other1 = (permuted(narrow1[:, 0:cut], 1), permuted(narrow1[:, cut:wide], 1))
    if groups == 2:
        nexts = (from_next_section(dx0), from_next_section(dx0, QUARTERS))
        next_back = nexts[0]
    else:
        total0 = dx0.astype(F32)
        for bit in range(2, groups.bit_length() + 1):
            total0 = total0 + permuted(total0, bit)
        nexts = (from_next_section(total0.astype(BF)),)
        next_back = jnp.where(lax.axis_index("dp") < QUARTERS, nexts[0], 0)

    def up1_body(*refs):
        next_refs, rest = refs[len(base):][:len(nexts)], refs[len(base) + len(nexts):]
        w2_ref, ys_ref, keep_ref, send_ref = rest
        core = lax.rem(lax.axis_index("dp"), 2)
        flat = joined(refs[:len(base)])
        row = iota((rows, n * used), 0)
        col = iota((rows, n * used), 1)
        want = place_of(row // CAP) * used + row % CAP
        value = dot(one_hot(col == want), flat)
        match = dot(one_hot(col == want + CAP), flat[:, 0:LANES])
        row = iota((rows, rows), 0)
        col = iota((rows, rows), 1)
        place = jnp.zeros((rows, rows), F32)
        for b in range(CAP):
            place = place + jnp.where(
                (row // CAP == col // CAP) & (col % CAP == b), match[:, b:b + 1], 0.0
            )
        for ref in next_refs:
            value = value + dot(place.astype(BF), ref[...])
        ys = value.astype(BF)
        ys_ref[...] = ys
        step = chunk_of(half, 512)
        for ref, which in ((send_ref, 1 - core), (keep_ref, core)):
            for at in range(0, half, step):
                lanes = pl.ds(pl.multiple_of(which * half + at, LANES), step)
                ref[:, at:at + step] = dot(ys, w2_ref[lanes, :], NT)

    ys1, keep1, send1 = call(
        up1_body,
        (*base, *nexts, w2),
        [VMEM] * (len(base) + len(nexts) + 1),
        (sds((rows, part), BF), sds((rows, half), F32), sds((rows, half), F32)),
        flops=2 * rows * part * hidden,
        data=2 * part * hidden,
    )
    send1, other1 = lax.optimization_barrier((send1, other1))
    up1 = keep1 + permuted(send1, 0)

    def act1_body(a_ref, low_ref, high_ref, out_ref, pre_ref, prob_ref):
        other = jnp.concatenate([low_ref[...], high_ref[...]], axis=1)
        prob = softmax_rows(all_logits(a_ref[...], other))
        pre = a_ref[:, 0:half] + other[:, 0:half].astype(F32)
        act, _ = silu_parts(pre)
        pre_ref[...] = pre
        out_ref[...] = (gate_of(prob) * act).astype(BF)
        prob_ref[...] = prob

    scaled1, pre1, prob1 = call(
        act1_body,
        (mine1, *other1),
        [VMEM] * 3,
        (sds((rows, half), BF), sds((rows, half), F32), sds((rows, LANES), F32)),
    )
    scaled1_pair = permuted(scaled1, 0)

    other_up1 = permuted(up1.astype(BF), 1)

    both = STEPS * rows

    def outer(body, args, height, across, rest):
        written = height - rest

        def write(*refs):
            a, b = body(*refs[:len(args)])
            out_ref, *rest_refs, held_ref, sems = refs[len(args):]
            step = written // SLAB
            copies = []
            for i in range(SLAB):
                at = pl.ds(i * step, step)
                held_ref[at, :] = dot(a[:, i * step:(i + 1) * step], b, TN).astype(BF)
                copies += copy_all(((held_ref.at[at], out_ref.at[at]),), sems.at[pl.ds(i, 1)])
            for ref in rest_refs:
                step = chunk_of(rest, 256)
                for i in range(0, rest, step):
                    ref[i:i + step, :] = dot(a[:, written + i:written + i + step], b, TN).astype(BF)
            wait_all(copies)

        result = call(
            write,
            args,
            [VMEM] * len(args),
            (sds((height, across), BF),) + ((pltpu.VMEM((rest, across), BF),) if rest else ()),
            flops=2 * both * height * across,
            data=2 * written * across,
            limit=16,
            out_specs=(ANY,) + ((VMEM,) if rest else ()),
            scratch=[pltpu.VMEM((written, across), BF), pltpu.SemaphoreType.DMA((SLAB,))],
        )
        return result if rest else result[0]

    def copy_rest(rest_ref, out_ref, sems):
        step = rest_ref.shape[0] // SLAB
        begin = out_ref.shape[0] - rest_ref.shape[0]
        return copy_all(
            [
                (rest_ref.at[pl.ds(i * step, step)], out_ref.at[pl.ds(begin + i * step, step)])
                for i in range(SLAB)
            ],
            sems,
        )

    def grad_out_body(own0, pair0, own1, pair1, ys0_ref, ys1_ref):
        core = lax.rem(lax.axis_index("dp"), 2)
        a0, b0 = in_order(own0[:, wide:wide + half], pair0[:, wide:wide + half], core)
        a1, b1 = in_order(own1[...], pair1[...], core)
        scaled = jnp.concatenate(
            [jnp.concatenate([a0, b0], axis=1), jnp.concatenate([a1, b1], axis=1)], axis=0
        )
        return scaled, jnp.concatenate([ys0_ref[...], ys1_ref[...]], axis=0)

    out_args = (hid0, hid0_pair, scaled1, scaled1_pair, ys0, ys1)
    grad_out, rest_out = outer(grad_out_body, out_args, hidden, part, half)

    other_up1, grad_out = lax.optimization_barrier((other_up1, grad_out))

    def act2_body(pre_ref, up_ref, other_ref, prob_ref, out_ref, block_ref):
        pre = pre_ref[...]
        upper = up_ref[...] + other_ref[...].astype(F32)
        _, dpre, block = gated(pre, upper, gate_of(prob_ref[...]))
        out_ref[:, 0:half] = dpre
        out_ref[:, half:wide] = split_sum(block)
        block_ref[...] = jnp.broadcast_to(block, (rows, LANES))

    hid1, block1 = call(
        act2_body,
        (pre1, up1, other_up1, prob1),
        [VMEM] * 4,
        (sds((rows, wide), BF), sds((rows, LANES), F32)),
    )
    hid1_pair = permuted(hid1, 0)

    back_rows = 2 * SLAB

    def dx1_body(
        own_ref, pair_ref, block_ref, prob_ref, dlog0_ref, dx0_ref, next_ref, xs_ref, router_ref, w1_ref, rest_ref, _, *refs
    ):
        grad_ref, *out_refs, sems = refs
        copies = copy_rest(rest_ref, grad_ref, sems)

        @pl.when(lax.axis_index("dp") >= 0)
        def _():
            core = lax.rem(lax.axis_index("dp"), 2)
            dx = dx_of(own_ref, pair_ref, w1_ref, core)
            dx, dlog = routed_back(dx, block_ref, pair_ref, prob_ref[...], router_ref)
            dlogs = jnp.concatenate([dlog0_ref[...], dlog], axis=0)
            grad = dot(
                jnp.concatenate(split3(dlogs), axis=0), jnp.concatenate([xs_ref[...]] * 3, axis=0), TN
            )[0:experts, :].astype(BF)
            source = jnp.concatenate([dx, dx0_ref[...], next_ref[...], grad], axis=0)
            count = 3 * rows + experts
            slabs = n // len(out_refs)
            row = iota((n * back_rows, count), 0)
            col = iota((n * back_rows, count), 1)
            home = row // back_rows
            if by_chip:
                home = place_of(home % slabs * 2 + home // slabs)
            kind = row % back_rows
            want = jnp.where(
                kind < 3 * CAP,
                (kind // CAP) * rows + home * CAP + kind % CAP,
                jnp.where(kind >= SLAB, 3 * rows + kind - SLAB, -1),
            )
            out = dot(one_hot(col == want), source).astype(BF)
            for i, ref in enumerate(out_refs):
                at = i * slabs * back_rows
                ref[...] = out[at:at + slabs * back_rows].reshape(slabs, back_rows, part)

        wait_all(copies)

    back_shapes = (sds((n // 2, back_rows, part), BF),) * 2 if by_chip else (sds((n, back_rows, part), BF),)
    grad_out, *back_sent = call(
        dx1_body,
        (hid1, hid1_pair, block1, prob1, dlog0, dx0, next_back, xs, router_q, w1, rest_out, grad_out),
        [VMEM] * 11 + [ANY],
        (sds((hidden, part), BF), *back_shapes),
        flops=2 * rows * part * hidden,
        data=2 * part * hidden,
        limit=12,
        out_specs=(ANY, *(VMEM for _ in back_shapes)),
        scratch=[pltpu.SemaphoreType.DMA((SLAB,))],
        aliases={11: 0},
    )
    if by_chip:
        back_handed = permuted(back_sent[1], 0)

        def pairs_body(mine_ref, handed_ref, *out_refs):
            for k, ref in enumerate(out_refs):
                ref[0] = mine_ref[k]
                ref[1] = handed_ref[k]

        chips = call(
            pairs_body,
            (back_sent[0], back_handed),
            [VMEM] * 2,
            tuple(sds((2, back_rows, part), BF) for _ in range(n // 2)),
        )
        back = tuple(exchanged(chip, 2 * k) if k else chip for k, chip in enumerate(chips))
    else:
        back = (lax.all_to_all(back_sent[0], "dp", split_axis=0, concat_axis=0, tiled=True),)

    def grad_in_body(own0, pair0, own1, pair1, xs_ref):
        core = lax.rem(lax.axis_index("dp"), 2)
        a0, b0 = in_order(own0[:, 0:half], pair0[:, 0:half], core)
        a1, b1 = in_order(own1[:, 0:half], pair1[:, 0:half], core)
        dpre = jnp.concatenate(
            [jnp.concatenate([a0, b0], axis=1), jnp.concatenate([a1, b1], axis=1)], axis=0
        )
        return xs_ref[...], dpre

    in_args = (hid0, hid0_pair, hid1, hid1_pair, xs)
    grad_in = outer(grad_in_body, in_args, part, hidden, 0)

    def final_body(ids_ref, counts_ref, dy_ref, onward_ref, head_ref, *refs):
        back_refs, (out_ref, router_out_ref) = refs[:-2], refs[-2:]
        section, dev = where_am_i()
        own = lax.rem(dev, QUARTERS)
        count = counts_ref[dev]
        last = section == last_section
        live0 = section < count
        live1 = 1 + section < count
        held0 = slot_tokens(ids_ref, 0, live0)
        held1 = slot_tokens(ids_ref, 1, live1)
        codes = onward_ref[tokens:tokens + 1, 0:LANES].astype(F32)
        before = [codes[:, c:c + 1] - 1.0 for c in range(CAP)]

        shape = (4 * SLAB, groups * back_rows)
        row = iota(shape, 0).astype(F32)
        col = lax.rem(iota(shape, 1), back_rows)
        place = (row - 3 * SLAB == (col - SLAB).astype(F32)) & (col >= SLAB)
        for i, (held, at) in enumerate(((held0, CAP), (before, 2 * CAP), (held1, 0))):
            for c in range(CAP):
                token = held[c].astype(F32)
                place = place | ((token >= 0) & (row == token + i * SLAB) & (col == at + c))
        place = one_hot(place)

        for i in range(QUARTERS):
            if by_chip:
                quarter = jnp.bitwise_xor(own, i)
                blocks = [back_refs[i // 2 + 2 * g][i % 2] for g in range(groups)]
            else:
                quarter = i
                blocks = [back_refs[0][g * QUARTERS + i] for g in range(groups)]
            lanes = pl.ds(pl.multiple_of(quarter * part, LANES), part)
            sums = dot(place, jnp.concatenate(blocks, axis=0))
            router_out_ref[:, lanes] = sums[3 * SLAB:3 * SLAB + experts]
            out0 = jnp.where(live0, dy_ref[:, lanes].astype(F32), 0.0) + sums[0:tokens]
            out1 = jnp.where(last, head_ref[:, lanes], onward_ref[0:tokens, lanes]).astype(F32)
            out1 = jnp.where(live1, out1, 0.0) + sums[SLAB:SLAB + tokens]
            out1 = out1.astype(BF).astype(F32) + sums[2 * SLAB:2 * SLAB + tokens]
            out0 = out0.astype(BF)
            out1 = out1.astype(BF)
            for t in range(tokens):
                out_ref[t, 0:1, lanes] = out0[t:t + 1]
                out_ref[t, 1:2, lanes] = out1[t:t + 1]

    grads, router_grad = call(
        final_body,
        (ids, replica_counts, carried_tok, onward, head_grad, *back),
        [SMEM, SMEM] + [VMEM] * (3 + len(back)),
        (sds((tokens, STEPS, width), BF), sds((experts, width), F32)),
        limit=24,
    )
    input_grad = grads.transpose(1, 0, 2)[:, None]
    return (input_grad, grad_in[None, None], grad_out[None, None], router_grad.T[None])


def solution(mesh):
    in_specs = (
        P("section", None, "dp", None),
        P("section", "dp", None),
        P("dp", None),
        P("section", None, "dp", None),
        P(),
        P("section", None, None),
        P("section", "dp", None, None),
        P("section", "dp", None, None),
    )
    out_specs = (
        P(None, "section", "dp", None),
        P("section", "dp", None, None),
        P("section", "dp", None, None),
        P("section", None, None),
    )
    return jax.shard_map(local, mesh=mesh, in_specs=in_specs, out_specs=out_specs, check_vma=False)
```

```python
import functools

import jax
import jax.numpy as jnp
from jax import lax
from jax.experimental import pallas as pl
from jax.experimental.pallas import tpu as pltpu
from jax.sharding import PartitionSpec as P

STEPS = 2
CAP = 2
QUARTERS = 4
LANES = 128
SLAB = 8
BF = jnp.bfloat16
F32 = jnp.float32
MIB = 1 << 20

NN = (((1,), (0,)), ((), ()))
NT = (((1,), (1,)), ((), ()))
TN = (((0,), (0,)), ((), ()))

VMEM = pl.BlockSpec(memory_space=pltpu.VMEM)
SMEM = pl.BlockSpec(memory_space=pltpu.SMEM)
ANY = pl.BlockSpec(memory_space=pl.ANY)


def dot(a, b, dims=NN):
    return lax.dot_general(a, b, dims, preferred_element_type=F32)


def split3(a):
    high = a.astype(BF)
    rest = a - high.astype(F32)
    mid = rest.astype(BF)
    return high, mid, (rest - mid.astype(F32)).astype(BF)


def dot_split(a, b, dims):
    at_a, at_b = dims[0][0][0], dims[0][1][0]
    a0, a1, a2 = split3(a)
    b0, b1, b2 = split3(b)
    return dot(
        jnp.concatenate([a0, a0, a1, a0, a1, a2], axis=at_a),
        jnp.concatenate([b0, b1, b0, b2, b1, b0], axis=at_b),
        dims,
    )


def iota(shape, dim):
    return lax.broadcasted_iota(jnp.int32, shape, dim)


def one_hot(cond):
    return jnp.where(cond, 1.0, 0.0).astype(BF)


def sds(shape, dtype):
    return jax.ShapeDtypeStruct(shape, dtype)


def call(body, args, specs, outs, flops=0, data=0, limit=12, scratch=(), out_specs=None, aliases=None):
    many = isinstance(outs, tuple)
    if out_specs is None:
        out_specs = tuple(VMEM for _ in outs) if many else VMEM
    return pl.pallas_call(
        body,
        in_specs=specs,
        out_specs=out_specs,
        out_shape=outs,
        scratch_shapes=scratch,
        input_output_aliases=aliases or {},
        cost_estimate=pl.CostEstimate(flops=flops, bytes_accessed=data, transcendentals=0),
        compiler_params=pltpu.CompilerParams(vmem_limit_bytes=limit * MIB),
    )(*args)


def in_hbm(array):
    return pltpu.with_memory_space_constraint(array, pltpu.HBM)


def copy_all(pairs, sems):
    copies = [
        pltpu.make_async_copy(source, target, sems.at[i])
        for i, (source, target) in enumerate(pairs)
    ]
    for copy in copies:
        copy.start()
    return copies


def wait_all(copies):
    for copy in copies:
        copy.wait()


def fetch(weight, columns):
    def body(source, target, sems):
        pieces = [pl.ds(start, size) for start, size in columns()]
        wait_all(copy_all([(source.at[:, at], target.at[:, at]) for at in pieces], sems))

    return call(
        body,
        (in_hbm(weight),),
        [ANY],
        pltpu.VMEM(weight.shape, weight.dtype),
        data=2 * weight.size,
        limit=4,
        scratch=[pltpu.SemaphoreType.DMA((SLAB,))],
    )


def chunk_of(size, most):
    while size % most:
        most //= 2
    return most


def exchanged(array, mask):
    count = lax.axis_size("dp")
    return lax.ppermute(array, "dp", [(i, i ^ mask) for i in range(count)])


def permuted(array, bit):
    return exchanged(array, 1 << bit)


def from_next_section(array, mask=0):
    count, devices = lax.axis_size("section"), lax.axis_size("dp")
    pairs = [
        (d * count + i + 1, (d ^ mask) * count + i) for d in range(devices) for i in range(count - 1)
    ]
    return lax.ppermute(array, ("dp", "section"), pairs)


def slot_tokens(ids, step, live):
    tokens = ids.shape[2]
    count = jnp.int32(0)
    held = [jnp.int32(-1)] * CAP
    for t in range(tokens):
        routed = ((ids[step, 0, t] == 0) | (ids[step, 1, t] == 0)) & live
        for c in range(CAP):
            held[c] = jnp.where(routed & (count == c), jnp.int32(t), held[c])
        count = count + routed.astype(jnp.int32)
    return held


def silu_parts(pre):
    sig = jax.nn.sigmoid(pre)
    return pre * sig, sig * (1.0 + pre * (1.0 - sig))


def softmax_rows(logits):
    expo = jnp.exp(logits)
    prob = expo / jnp.sum(expo, axis=1, keepdims=True)
    rows, experts = logits.shape
    return jnp.concatenate([prob, jnp.zeros((rows, LANES - experts), F32)], axis=1)


def first_minus(prob):
    lane = iota(prob.shape, 1)
    return jnp.where(lane == 0, 1.0, 0.0) - prob


def local(saved_inputs, carried, head_grad, routing, replica_counts, router, w_in, w_out):
    sections = lax.axis_size("section")
    n = lax.axis_size("dp")
    groups = n // QUARTERS
    width = head_grad.shape[1]
    tokens = head_grad.shape[0]
    part = w_in.shape[2]
    hidden = w_in.shape[3]
    half = hidden // 2
    experts = router.shape[2]
    rows = n * CAP
    router_t = router[0].T
    x_tok = saved_inputs[0].transpose(1, 0, 2)
    carried_tok = carried[0]
    ids = routing[0].transpose(0, 2, 1)
    last_section = sections - 1
    step = chunk_of(half, 512)
    late = half // step // 2 * step

    def early_columns():
        core = lax.rem(lax.axis_index("dp"), 2)
        send = pl.multiple_of((1 - core) * half, LANES)
        keep = pl.multiple_of(core * half, LANES)
        return [(send, half)] + ([(keep, half - late)] if late < half else [])

    w1 = fetch(w_in[0, 0], early_columns)

    def where_am_i():
        return lax.axis_index("section"), lax.axis_index("dp")

    def quarter_lanes():
        return pl.ds(pl.multiple_of(lax.rem(lax.axis_index("dp"), QUARTERS) * part, LANES), part)

    def half_lanes(core):
        return pl.ds(pl.multiple_of(core * half, LANES), half)

    def pick(held, value):
        row = iota((SLAB, value.shape[0]), 0)
        col = iota((SLAB, value.shape[0]), 1)
        chosen = jnp.zeros((SLAB, value.shape[0]), F32)
        for c in range(len(held)):
            chosen = chosen + jnp.where((row == c) & (col == held[c]), 1.0, 0.0)
        return dot(chosen.astype(BF), value)

    by_chip = n == 2 * QUARTERS

    def place_of(home):
        return jnp.bitwise_xor(home, lax.axis_index("dp")) if by_chip else home

    def send_quarters(slab_ref, slab, mine_ref, theirs_ref):
        slab_ref[...] = slab
        own = lax.rem(lax.axis_index("dp"), QUARTERS)
        for i in range(QUARTERS):
            at = pl.multiple_of(jnp.bitwise_xor(own, i) * part, LANES)
            ref = theirs_ref if i % 2 else mine_ref
            ref[i // 2] = slab_ref[:, pl.ds(at, part)].astype(BF)

    send_shapes = (sds((2, SLAB, part), BF), sds((2, SLAB, part), BF))
    slab_scratch = pltpu.VMEM((SLAB, width), F32)

    def spread_whole(mine, theirs):
        own = lax.rem(lax.axis_index("dp"), QUARTERS)
        quads = jnp.stack([mine[0], theirs[0], mine[1], theirs[1]])
        block = quads[jnp.bitwise_xor(jnp.arange(n) % QUARTERS, own)]
        return (lax.all_to_all(block, "dp", split_axis=0, concat_axis=0, tiled=True),)

    def spread_in_chip(mine, theirs):
        handed = permuted(theirs, 0)
        return jnp.stack([mine[0], handed[0]]), jnp.stack([mine[1], handed[1]])

    def joined(refs):
        return jnp.concatenate([ref[...].reshape(-1, part) for ref in refs], axis=0)

    def dispatch_body(
        ids_hbm,
        counts_hbm,
        x_hbm,
        dy_hbm,
        mine_ref,
        theirs_ref,
        onward_ref,
        ids_ref,
        counts_ref,
        x_ref,
        dy_ref,
        slab_ref,
        sems,
    ):
        wait_all(
            copy_all(
                ((ids_hbm, ids_ref), (counts_hbm, counts_ref), (dy_hbm, dy_ref), (x_hbm, x_ref)),
                sems,
            )
        )
        section, dev = where_am_i()
        count = counts_ref[dev]
        held = [slot_tokens(ids_ref, step, step + section < count) for step in range(STEPS)]
        dy = dy_ref[...]
        slab = pick([-1] * (STEPS * CAP) + held[0], dy)
        row = iota((SLAB, width), 0)
        lane = lax.rem(iota((SLAB, width), 1), part)
        for step in range(STEPS):
            for c in range(CAP):
                value = x_ref[jnp.maximum(held[step][c], 0), step:step + 1, :].astype(F32)
                wanted = (row == step * CAP + c) & (held[step][c] >= 0)
                slab = jnp.where(wanted, jnp.broadcast_to(value, (SLAB, width)), slab)
        send_quarters(slab_ref, slab, mine_ref, theirs_ref)
        onward = pick(list(range(tokens)), dy)
        for c in range(CAP):
            code = (held[0][c] + 1).astype(F32)
            onward = jnp.where((row == tokens) & (lane == c), code, onward)
        onward_ref[...] = onward.astype(BF)

    mine, theirs, onward = call(
        dispatch_body,
        (in_hbm(ids), in_hbm(replica_counts), in_hbm(x_tok), in_hbm(carried_tok)),
        [ANY] * 4,
        (*send_shapes, sds((SLAB, width), BF)),
        data=4 * MIB,
        scratch=[
            pltpu.SMEM(ids.shape, jnp.int32),
            pltpu.SMEM(replica_counts.shape, jnp.int32),
            pltpu.VMEM(x_tok.shape, BF),
            pltpu.VMEM(carried_tok.shape, BF),
            slab_scratch,
            pltpu.SemaphoreType.DMA((4,)),
        ],
    )
    onward = from_next_section(onward)
    if by_chip:
        same, cross = spread_in_chip(mine, theirs)
        came = (same, exchanged(cross, 2), exchanged(same, 4), exchanged(cross, 6))
    else:
        came = spread_whole(mine, theirs)
    came, onward = lax.optimization_barrier((came, onward))

    wide = half + LANES

    def first_body(*refs):
        w1_hbm, _, w2_hbm, router_hbm, *refs_out = refs[len(came):]
        w1_ref, xs_ref, ys_ref, keep_ref, send_ref, w2_ref, router_ref, sems = refs_out
        core = lax.rem(lax.axis_index("dp"), 2)
        router_copy = pltpu.make_async_copy(
            router_hbm.at[:, quarter_lanes()], router_ref, sems.at[0]
        )
        router_copy.start()
        late_at = pl.ds(pl.multiple_of(core * half + half - late, LANES), late) if late else None
        late_copies = copy_all(
            [(w1_hbm.at[:, late_at], w1_ref.at[:, late_at])] if late else [], sems.at[pl.ds(1, 1)]
        )
        chunks = [
            (ref, at, pl.multiple_of(which * half + at, LANES))
            for ref, which in ((send_ref, 1 - core), (keep_ref, core))
            for at in range(0, half, step)
        ]
        copies = copy_all(
            [(w2_hbm.at[pl.ds(lane, step)], w2_ref.at[pl.ds(lane, step)]) for _, _, lane in chunks],
            sems.at[pl.ds(2, len(chunks))],
        )

        @pl.when(lax.axis_index("dp") >= 0)
        def _():
            flat = joined(refs[:len(came)])
            row = iota((STEPS * rows, n * SLAB), 0)
            col = iota((STEPS * rows, n * SLAB), 1)
            slot = row % rows
            want = place_of(slot // CAP) * SLAB + (row // rows) * CAP + slot % CAP
            xs = dot(one_hot(col == want), flat).astype(BF)
            row = iota((rows, n * SLAB), 0)
            col = iota((rows, n * SLAB), 1)
            ys = dot(one_hot(col == place_of(row // CAP) * SLAB + 2 * CAP + row % CAP), flat).astype(BF)
            xs_ref[...] = xs
            ys_ref[...] = ys
            router_copy.wait()
            parts = jnp.concatenate(
                [
                    jnp.concatenate([p, jnp.zeros((LANES - experts, part), BF)], axis=0)
                    for p in split3(router_ref[...])
                ],
                axis=0,
            )
            logits = dot(xs, parts, NT)
            logits = logits[:, 0:LANES] + logits[:, LANES:2 * LANES] + logits[:, 2 * LANES:3 * LANES]
            zero = jnp.zeros((rows, LANES), F32)
            both = STEPS * rows
            for i, (ref, at, lane) in enumerate(chunks):
                if i == len(chunks) - late // step:
                    wait_all(late_copies)
                ref[0:both, at:at + step] = dot(xs, w1_ref[:, pl.ds(lane, step)])
            for ref in (send_ref, keep_ref):
                ref[0:both, half:wide] = logits
                ref[both:both + rows, half:wide] = zero
            for (ref, at, lane), copy in zip(chunks, copies):
                copy.wait()
                ref[both:both + rows, at:at + step] = dot(ys, w2_ref[pl.ds(lane, step), :], NT)

    w1, xs, ys0, keep, send, w2, router_q = call(
        first_body,
        (*came, in_hbm(w_in[0, 0]), w1, in_hbm(w_out[0, 0]), in_hbm(router_t)),
        [VMEM] * len(came) + [ANY, VMEM, ANY, ANY],
        (
            pltpu.VMEM((part, hidden), BF),
            sds((STEPS * rows, part), BF),
            sds((rows, part), BF),
            sds((3 * rows, wide), F32),
            sds((3 * rows, wide), F32),
            pltpu.VMEM((hidden, part), BF),
            sds((experts, part), F32),
        ),
        flops=2 * 3 * rows * part * hidden,
        data=2 * part * hidden * 2,
        scratch=[pltpu.SemaphoreType.DMA((2 + 2 * (half // step),))],
        aliases={len(came) + 1: 0},
    )
    send, onward = lax.optimization_barrier((send, onward))
    send_other = permuted(send, 0)

    def base_body(
        ids_hbm,
        counts_hbm,
        onward_ref,
        head_hbm,
        mine_ref,
        theirs_ref,
        ids_ref,
        counts_ref,
        head_ref,
        slab_ref,
        sems,
    ):
        wait_all(
            copy_all(((ids_hbm, ids_ref), (counts_hbm, counts_ref), (head_hbm, head_ref)), sems)
        )
        section, dev = where_am_i()
        live = 1 + section < counts_ref[dev]
        last = section == last_section
        held = slot_tokens(ids_ref, 1, live)
        onward = onward_ref[...]
        slab = pick(held, jnp.where(last, head_ref[...], onward[0:tokens]))
        row = iota((SLAB, width), 0)
        code = jnp.broadcast_to(onward[tokens:tokens + 1].astype(F32), (SLAB, width))
        for c in range(CAP):
            same = (held[c] >= 0) & (code == (held[c] + 1).astype(F32))
            slab = jnp.where((row == CAP + c) & same, 1.0, slab)
        send_quarters(slab_ref, slab, mine_ref, theirs_ref)

    base_sent = call(
        base_body,
        (in_hbm(ids), in_hbm(replica_counts), onward, in_hbm(head_grad)),
        [ANY, ANY, VMEM, ANY],
        send_shapes,
        data=4 * MIB,
        scratch=[
            pltpu.SMEM(ids.shape, jnp.int32),
            pltpu.SMEM(replica_counts.shape, jnp.int32),
            pltpu.VMEM(head_grad.shape, BF),
            slab_scratch,
            pltpu.SemaphoreType.DMA((3,)),
        ],
    )
    send_other, base_sent = lax.optimization_barrier((send_other, base_sent))

    def pair_body(keep_ref, other_ref, mine0_ref, mine1_ref, narrow0_ref, narrow1_ref):
        both = STEPS * rows
        for at, ref, narrow, to in (
            (0, mine0_ref, narrow0_ref, 0),
            (both, mine0_ref, narrow0_ref, rows),
            (rows, mine1_ref, narrow1_ref, 0),
        ):
            total = keep_ref[at:at + rows, :] + other_ref[at:at + rows, :]
            ref[to:to + rows, :] = total
            narrow[to:to + rows, 0:half] = total[:, 0:half].astype(BF)
            pieces = split3(total[:, half:half + experts])
            spare = jnp.zeros((rows, LANES - 3 * experts), BF)
            narrow[to:to + rows, half:wide] = jnp.concatenate([*pieces, spare], axis=1)

    mine0, mine1, narrow0, narrow1 = call(
        pair_body,
        (keep, send_other),
        [VMEM] * 2,
        (
            sds((2 * rows, wide), F32),
            sds((rows, wide), F32),
            sds((2 * rows, wide), BF),
            sds((rows, wide), BF),
        ),
    )
    other0 = permuted(narrow0, 1)

    used = 2 * CAP
    if by_chip:
        base_handed = permuted(base_sent[1], 0)

        def join_body(mine_ref, handed_ref, same_ref, cross_ref):
            for i, ref in enumerate((same_ref, cross_ref)):
                ref[...] = jnp.concatenate([mine_ref[i, 0:used], handed_ref[i, 0:used]], axis=0)

        base_same, base_cross = call(
            join_body,
            (base_sent[0], base_handed),
            [VMEM] * 2,
            (sds((2 * used, part), BF), sds((2 * used, part), BF)),
        )
        base_beside = exchanged(base_cross, 2)
        other0, base_beside = lax.optimization_barrier((other0, base_beside))

        def four_body(same_ref, beside_ref, out_ref):
            out_ref[...] = jnp.concatenate([same_ref[...], beside_ref[...]], axis=0)

        base_four = call(four_body, (base_same, base_beside), [VMEM] * 2, sds((4 * used, part), BF))
    else:
        base_whole = spread_whole(*base_sent)[0][:, 0:used]

    def all_logits(own, other):
        at = half + experts
        pieces = [other[:, half + i * experts:at + i * experts].astype(F32) for i in range(3)]
        return own[:, half:at] + (pieces[0] + pieces[1] + pieces[2])

    def gated(pre, upper, gate):
        act, slope = silu_parts(pre)
        dpre = (gate * upper * slope).astype(BF)
        block = jnp.sum(act * upper, axis=1, keepdims=True)
        return act, dpre, block

    def split_sum(block):
        high = block.astype(BF)
        low = (block - high.astype(F32)).astype(BF)
        lane = iota((rows, LANES), 1)
        zero = jnp.zeros((rows, LANES), BF)
        return jnp.where(lane == 0, high, jnp.where(lane == 1, low, zero))

    def gate_of(prob):
        return prob[:, 0:1].astype(BF).astype(F32)

    def act0_body(a_ref, b_ref, out_ref, prob_ref, block_ref):
        total = a_ref[:, 0:half] + b_ref[:, 0:half].astype(F32)
        prob = softmax_rows(all_logits(a_ref[0:rows, :], b_ref[0:rows, :]))
        gate = gate_of(prob)
        pre = total[0:rows]
        upper = total[rows:2 * rows]
        act, dpre, block = gated(pre, upper, gate)
        out_ref[:, 0:half] = dpre
        out_ref[:, half:wide] = split_sum(block)
        out_ref[:, wide:wide + half] = (gate * act).astype(BF)
        prob_ref[...] = prob
        block_ref[...] = jnp.broadcast_to(block, (rows, LANES))

    hid0, prob0, block0 = call(
        act0_body,
        (mine0, other0),
        [VMEM] * 2,
        (sds((rows, wide + half), BF), sds((rows, LANES), F32), sds((rows, LANES), F32)),
    )
    hid0_pair = permuted(hid0, 0)

    def block_sum(block, pair_ref):
        extra = pair_ref[:, half:half + 1].astype(F32) + pair_ref[:, half + 1:half + 2].astype(F32)
        return (block[:, 0:1] + extra).astype(BF)

    def in_order(own, pair, core):
        return (
            jnp.where(core == 0, own, pair),
            jnp.where(core == 0, pair, own),
        )

    def dx_of(own_ref, pair_ref, w1_ref, core):
        low, high = in_order(own_ref[:, 0:half], pair_ref[:, 0:half], core)
        step = chunk_of(part, 256)
        pieces = []
        for at in range(0, part, step):
            pieces.append(
                dot(low, w1_ref[at:at + step, 0:half], NT)
                + dot(high, w1_ref[at:at + step, half:hidden], NT)
            )
        return jnp.concatenate(pieces, axis=1)

    def routed_back(dx, block_ref, pair_ref, prob, router_ref):
        dgate = block_sum(block_ref[...], pair_ref).astype(F32)
        dlog = dgate * prob[:, 0:1] * first_minus(prob)
        return (dx + dot_split(dlog[:, 0:experts], router_ref[...], NN)).astype(BF), dlog

    def dx0_body(own_ref, pair_ref, block_ref, prob_ref, router_ref, w1_ref, out_ref, dlog_ref):
        core = lax.rem(lax.axis_index("dp"), 2)
        dx = dx_of(own_ref, pair_ref, w1_ref, core)
        out_ref[...], dlog_ref[...] = routed_back(dx, block_ref, pair_ref, prob_ref[...], router_ref)

    dx0, dlog0 = call(
        dx0_body,
        (hid0, hid0_pair, block0, prob0, router_q, w1),
        [VMEM] * 6,
        (sds((rows, part), BF), sds((rows, LANES), F32)),
        flops=2 * rows * part * hidden,
        data=2 * part * hidden,
    )
    if by_chip:
        base_far = exchanged(base_four, 4)
        dx0, narrow1, base_far = lax.optimization_barrier((dx0, narrow1, base_far))
        base = (base_four, base_far)
    else:
        base = (base_whole.reshape(n * used, part),)
    cut = half // 2
    other1 = (permuted(narrow1[:, 0:cut], 1), permuted(narrow1[:, cut:wide], 1))
    if groups == 2:
        nexts = (from_next_section(dx0), from_next_section(dx0, QUARTERS))
        next_back = nexts[0]
    else:
        total0 = dx0.astype(F32)
        for bit in range(2, groups.bit_length() + 1):
            total0 = total0 + permuted(total0, bit)
        nexts = (from_next_section(total0.astype(BF)),)
        next_back = jnp.where(lax.axis_index("dp") < QUARTERS, nexts[0], 0)

    def up1_body(*refs):
        next_refs, rest = refs[len(base):][:len(nexts)], refs[len(base) + len(nexts):]
        w2_ref, ys_ref, keep_ref, send_ref = rest
        core = lax.rem(lax.axis_index("dp"), 2)
        flat = joined(refs[:len(base)])
        row = iota((rows, n * used), 0)
        col = iota((rows, n * used), 1)
        want = place_of(row // CAP) * used + row % CAP
        value = dot(one_hot(col == want), flat)
        match = dot(one_hot(col == want + CAP), flat[:, 0:LANES])
        row = iota((rows, rows), 0)
        col = iota((rows, rows), 1)
        place = jnp.zeros((rows, rows), F32)
        for b in range(CAP):
            place = place + jnp.where(
                (row // CAP == col // CAP) & (col % CAP == b), match[:, b:b + 1], 0.0
            )
        for ref in next_refs:
            value = value + dot(place.astype(BF), ref[...])
        ys = value.astype(BF)
        ys_ref[...] = ys
        step = chunk_of(half, 512)
        for ref, which in ((send_ref, 1 - core), (keep_ref, core)):
            for at in range(0, half, step):
                lanes = pl.ds(pl.multiple_of(which * half + at, LANES), step)
                ref[:, at:at + step] = dot(ys, w2_ref[lanes, :], NT)

    ys1, keep1, send1 = call(
        up1_body,
        (*base, *nexts, w2),
        [VMEM] * (len(base) + len(nexts) + 1),
        (sds((rows, part), BF), sds((rows, half), F32), sds((rows, half), F32)),
        flops=2 * rows * part * hidden,
        data=2 * part * hidden,
    )
    send1, other1 = lax.optimization_barrier((send1, other1))
    up1 = keep1 + permuted(send1, 0)

    def act1_body(a_ref, low_ref, high_ref, out_ref, pre_ref, prob_ref):
        other = jnp.concatenate([low_ref[...], high_ref[...]], axis=1)
        prob = softmax_rows(all_logits(a_ref[...], other))
        pre = a_ref[:, 0:half] + other[:, 0:half].astype(F32)
        act, _ = silu_parts(pre)
        pre_ref[...] = pre
        out_ref[...] = (gate_of(prob) * act).astype(BF)
        prob_ref[...] = prob

    scaled1, pre1, prob1 = call(
        act1_body,
        (mine1, *other1),
        [VMEM] * 3,
        (sds((rows, half), BF), sds((rows, half), F32), sds((rows, LANES), F32)),
    )
    scaled1_pair = permuted(scaled1, 0)

    other_up1 = permuted(up1.astype(BF), 1)

    both = STEPS * rows

    def outer(body, args, height, across, rest):
        written = height - rest

        def write(*refs):
            a, b = body(*refs[:len(args)])
            out_ref, *rest_refs, held_ref, sems = refs[len(args):]
            step = written // SLAB
            copies = []
            for i in range(SLAB):
                at = pl.ds(i * step, step)
                held_ref[at, :] = dot(a[:, i * step:(i + 1) * step], b, TN).astype(BF)
                copies += copy_all(((held_ref.at[at], out_ref.at[at]),), sems.at[pl.ds(i, 1)])
            for ref in rest_refs:
                step = chunk_of(rest, 256)
                for i in range(0, rest, step):
                    ref[i:i + step, :] = dot(a[:, written + i:written + i + step], b, TN).astype(BF)
            wait_all(copies)

        result = call(
            write,
            args,
            [VMEM] * len(args),
            (sds((height, across), BF),) + ((pltpu.VMEM((rest, across), BF),) if rest else ()),
            flops=2 * both * height * across,
            data=2 * written * across,
            limit=16,
            out_specs=(ANY,) + ((VMEM,) if rest else ()),
            scratch=[pltpu.VMEM((written, across), BF), pltpu.SemaphoreType.DMA((SLAB,))],
        )
        return result if rest else result[0]

    def copy_rest(rest_ref, out_ref, sems):
        step = rest_ref.shape[0] // SLAB
        begin = out_ref.shape[0] - rest_ref.shape[0]
        return copy_all(
            [
                (rest_ref.at[pl.ds(i * step, step)], out_ref.at[pl.ds(begin + i * step, step)])
                for i in range(SLAB)
            ],
            sems,
        )

    def grad_out_body(own0, pair0, own1, pair1, ys0_ref, ys1_ref):
        core = lax.rem(lax.axis_index("dp"), 2)
        a0, b0 = in_order(own0[:, wide:wide + half], pair0[:, wide:wide + half], core)
        a1, b1 = in_order(own1[...], pair1[...], core)
        scaled = jnp.concatenate(
            [jnp.concatenate([a0, b0], axis=1), jnp.concatenate([a1, b1], axis=1)], axis=0
        )
        return scaled, jnp.concatenate([ys0_ref[...], ys1_ref[...]], axis=0)

    out_args = (hid0, hid0_pair, scaled1, scaled1_pair, ys0, ys1)
    grad_out, rest_out = outer(grad_out_body, out_args, hidden, part, half)

    other_up1, grad_out = lax.optimization_barrier((other_up1, grad_out))

    def act2_body(pre_ref, up_ref, other_ref, prob_ref, out_ref, block_ref):
        pre = pre_ref[...]
        upper = up_ref[...] + other_ref[...].astype(F32)
        _, dpre, block = gated(pre, upper, gate_of(prob_ref[...]))
        out_ref[:, 0:half] = dpre
        out_ref[:, half:wide] = split_sum(block)
        block_ref[...] = jnp.broadcast_to(block, (rows, LANES))

    hid1, block1 = call(
        act2_body,
        (pre1, up1, other_up1, prob1),
        [VMEM] * 4,
        (sds((rows, wide), BF), sds((rows, LANES), F32)),
    )
    hid1_pair = permuted(hid1, 0)

    first_rows = part // 2

    def early_in_body(own0, own1, xs_ref, out_ref):
        dpre = jnp.concatenate([own0[:, 0:half], own1[:, 0:half]], axis=0)
        rows_at = chunk_of(first_rows, 256)
        for i in range(0, first_rows, rows_at):
            out_ref[i:i + rows_at, :] = dot(xs_ref[:, i:i + rows_at], dpre, TN).astype(BF)

    early_in = call(
        early_in_body,
        (hid0, hid1, xs),
        [VMEM] * 3,
        pltpu.VMEM((first_rows, half), BF),
        flops=2 * both * first_rows * half,
        data=2 * first_rows * half,
    )

    back_rows = 2 * SLAB

    def dx1_body(
        own_ref, pair_ref, block_ref, prob_ref, dlog0_ref, dx0_ref, next_ref, xs_ref, router_ref, w1_ref, rest_ref, _, *refs
    ):
        early_ref, grad_ref, grad_in_ref, *out_refs, sems = refs
        copies = copy_rest(rest_ref, grad_ref, sems.at[pl.ds(0, SLAB)])
        own_lanes = half_lanes(lax.rem(lax.axis_index("dp"), 2))
        step = first_rows // SLAB
        some = [pl.ds(i * step, step) for i in range(SLAB)]
        copies += copy_all(
            [(early_ref.at[at], grad_in_ref.at[at, own_lanes]) for at in some], sems.at[pl.ds(SLAB, SLAB)]
        )

        @pl.when(lax.axis_index("dp") >= 0)
        def _():
            core = lax.rem(lax.axis_index("dp"), 2)
            dx = dx_of(own_ref, pair_ref, w1_ref, core)
            dx, dlog = routed_back(dx, block_ref, pair_ref, prob_ref[...], router_ref)
            dlogs = jnp.concatenate([dlog0_ref[...], dlog], axis=0)
            grad = dot(
                jnp.concatenate(split3(dlogs), axis=0), jnp.concatenate([xs_ref[...]] * 3, axis=0), TN
            )[0:experts, :].astype(BF)
            source = jnp.concatenate([dx, dx0_ref[...], next_ref[...], grad], axis=0)
            count = 3 * rows + experts
            slabs = n // len(out_refs)
            row = iota((n * back_rows, count), 0)
            col = iota((n * back_rows, count), 1)
            home = row // back_rows
            if by_chip:
                home = place_of(home % slabs * 2 + home // slabs)
            kind = row % back_rows
            want = jnp.where(
                kind < 3 * CAP,
                (kind // CAP) * rows + home * CAP + kind % CAP,
                jnp.where(kind >= SLAB, 3 * rows + kind - SLAB, -1),
            )
            out = dot(one_hot(col == want), source).astype(BF)
            for i, ref in enumerate(out_refs):
                at = i * slabs * back_rows
                ref[...] = out[at:at + slabs * back_rows].reshape(slabs, back_rows, part)

        wait_all(copies)

    back_shapes = (sds((n // 2, back_rows, part), BF),) * 2 if by_chip else (sds((n, back_rows, part), BF),)
    grad_out, grad_in, *back_sent = call(
        dx1_body,
        (hid1, hid1_pair, block1, prob1, dlog0, dx0, next_back, xs, router_q, w1, rest_out, grad_out, early_in),
        [VMEM] * 11 + [ANY, VMEM],
        (sds((hidden, part), BF), sds((part, hidden), BF), *back_shapes),
        flops=2 * rows * part * hidden,
        data=2 * part * hidden,
        limit=12,
        out_specs=(ANY, ANY, *(VMEM for _ in back_shapes)),
        scratch=[pltpu.SemaphoreType.DMA((2 * SLAB,))],
        aliases={11: 0},
    )
    if by_chip:
        back_handed = permuted(back_sent[1], 0)

        def pairs_body(mine_ref, handed_ref, *out_refs):
            for k, ref in enumerate(out_refs):
                ref[0] = mine_ref[k]
                ref[1] = handed_ref[k]

        chips = call(
            pairs_body,
            (back_sent[0], back_handed),
            [VMEM] * 2,
            tuple(sds((2, back_rows, part), BF) for _ in range(n // 2)),
        )
        back = tuple(exchanged(chip, 2 * k) if k else chip for k, chip in enumerate(chips))
    else:
        back = (lax.all_to_all(back_sent[0], "dp", split_axis=0, concat_axis=0, tiled=True),)

    def grad_in_body(own0, pair0, own1, pair1, xs_ref, _, out_ref, held_ref, narrow_ref, sems):
        core = lax.rem(lax.axis_index("dp"), 2)
        pair = jnp.concatenate([pair0[:, 0:half], pair1[:, 0:half]], axis=0)
        own = jnp.concatenate([own0[:, 0:half], own1[:, 0:half]], axis=0)
        dpre = jnp.concatenate(in_order(own, pair, core), axis=1)
        step = first_rows // (SLAB // 2)
        copies = []
        for i in range(SLAB // 2):
            begin = i * step
            narrow_ref[begin:begin + step, :] = dot(xs_ref[:, begin:begin + step], pair, TN).astype(BF)
            at = pl.ds(begin, step)
            target = out_ref.at[at, half_lanes(1 - core)]
            copies += copy_all([(narrow_ref.at[at], target)], sems.at[pl.ds(i, 1)])
        step = (part - first_rows) // (SLAB // 2)
        for i in range(SLAB // 2):
            begin = i * step
            rows_at = first_rows + begin
            held_ref[begin:begin + step, :] = dot(
                xs_ref[:, rows_at:rows_at + step], dpre, TN
            ).astype(BF)
            pair_of = (held_ref.at[pl.ds(begin, step)], out_ref.at[pl.ds(rows_at, step)])
            copies += copy_all([pair_of], sems.at[pl.ds(SLAB // 2 + i, 1)])
        wait_all(copies)

    grad_in = call(
        grad_in_body,
        (hid0, hid0_pair, hid1, hid1_pair, xs, grad_in),
        [VMEM] * 5 + [ANY],
        sds((part, hidden), BF),
        flops=2 * both * part * hidden,
        data=2 * part * hidden,
        limit=16,
        out_specs=ANY,
        scratch=[
            pltpu.VMEM((part - first_rows, hidden), BF),
            pltpu.VMEM((first_rows, half), BF),
            pltpu.SemaphoreType.DMA((SLAB,)),
        ],
        aliases={5: 0},
    )

    def final_body(ids_ref, counts_ref, dy_ref, onward_ref, head_ref, *refs):
        back_refs, (out_ref, router_out_ref) = refs[:-2], refs[-2:]
        section, dev = where_am_i()
        own = lax.rem(dev, QUARTERS)
        count = counts_ref[dev]
        last = section == last_section
        live0 = section < count
        live1 = 1 + section < count
        held0 = slot_tokens(ids_ref, 0, live0)
        held1 = slot_tokens(ids_ref, 1, live1)
        codes = onward_ref[tokens:tokens + 1, 0:LANES].astype(F32)
        before = [codes[:, c:c + 1] - 1.0 for c in range(CAP)]

        shape = (4 * SLAB, groups * back_rows)
        row = iota(shape, 0).astype(F32)
        col = lax.rem(iota(shape, 1), back_rows)
        place = (row - 3 * SLAB == (col - SLAB).astype(F32)) & (col >= SLAB)
        for i, (held, at) in enumerate(((held0, CAP), (before, 2 * CAP), (held1, 0))):
            for c in range(CAP):
                token = held[c].astype(F32)
                place = place | ((token >= 0) & (row == token + i * SLAB) & (col == at + c))
        place = one_hot(place)

        for i in range(QUARTERS):
            if by_chip:
                quarter = jnp.bitwise_xor(own, i)
                blocks = [back_refs[i // 2 + 2 * g][i % 2] for g in range(groups)]
            else:
                quarter = i
                blocks = [back_refs[0][g * QUARTERS + i] for g in range(groups)]
            lanes = pl.ds(pl.multiple_of(quarter * part, LANES), part)
            sums = dot(place, jnp.concatenate(blocks, axis=0))
            router_out_ref[:, lanes] = sums[3 * SLAB:3 * SLAB + experts]
            out0 = jnp.where(live0, dy_ref[:, lanes].astype(F32), 0.0) + sums[0:tokens]
            out1 = jnp.where(last, head_ref[:, lanes], onward_ref[0:tokens, lanes]).astype(F32)
            out1 = jnp.where(live1, out1, 0.0) + sums[SLAB:SLAB + tokens]
            out1 = out1.astype(BF).astype(F32) + sums[2 * SLAB:2 * SLAB + tokens]
            out0 = out0.astype(BF)
            out1 = out1.astype(BF)
            for t in range(tokens):
                out_ref[t, 0:1, lanes] = out0[t:t + 1]
                out_ref[t, 1:2, lanes] = out1[t:t + 1]

    grads, router_grad = call(
        final_body,
        (ids, replica_counts, carried_tok, onward, head_grad, *back),
        [SMEM, SMEM] + [VMEM] * (3 + len(back)),
        (sds((tokens, STEPS, width), BF), sds((experts, width), F32)),
        limit=24,
    )
    input_grad = grads.transpose(1, 0, 2)[:, None]
    return (input_grad, grad_in[None, None], grad_out[None, None], router_grad.T[None])


def solution(mesh):
    in_specs = (
        P("section", None, "dp", None),
        P("section", "dp", None),
        P("dp", None),
        P("section", None, "dp", None),
        P(),
        P("section", None, None),
        P("section", "dp", None, None),
        P("section", "dp", None, None),
    )
    out_specs = (
        P(None, "section", "dp", None),
        P("section", "dp", None, None),
        P("section", "dp", None, None),
        P("section", None, None),
    )
    return jax.shard_map(local, mesh=mesh, in_specs=in_specs, out_specs=out_specs, check_vma=False)
```
